128 devices in a mesh: replica: 8 (over y, x_lo), fsdp: 16 (over z, x_hi, core).
Axes of the slice: x: 4 (x_hi: 2, x_lo: 2; x = x_hi * 2 + x_lo), y: 4, z: 4, core: 2. Of those that a mesh axis runs over, the one named last changes fastest.
Arguments:
- tokens: bfloat16 [8, 12288, 8192], P('replica', 'fsdp'), may hold values from -6 to 6
- gain: float32 [8, 8192], P('replica'), may hold values from 0.1 to 1.9
- next_weights: bfloat16 [8, 8192, 1024], P('replica', 'fsdp'), may hold values from -0.0625 to 0.0625
- weights: bfloat16 [8, 8192, 1024], P('replica', 'fsdp'), may hold values from -6 to 6
- snapshot: float32 [8192, 1024], P('fsdp'), may hold values from -6 to 6
- momentum: bfloat16 [8192, 1024], P('fsdp', 'replica'), may hold values from -3 to 3
Outputs:
- next_keys: bfloat16 [8, 12288, 1024], P('replica', 'fsdp')
- new_weights: bfloat16 [8192, 1024], P('fsdp')
- new_momentum: bfloat16 [8192, 1024], P('fsdp', 'replica')
The draws below stay inside these ranges and needn't reach their ends.
All inputs are finite; a program needn't handle non-finite values.
Results may differ from the reference program's by a relative error of at most 0.015.
Values may be sent and summed in bfloat16 or wider, within the bound.
No kernel may reach another device: no remote copies, remote signals or barrier semaphores. Data moves between devices by JAX's collectives and lax.ppermute only.
A program may use at most 128 MiB of HBM per device.

```python
import jax
import jax.numpy as jnp
from jax import lax

D = 8192
KV = 1024
BLOCK = 128
TOKENS = 12288
REPLICAS = 8


def level_of(stream_key, dims, cuts, low, high):
    def one(dim, blocks):
        steps = jax.random.uniform(jax.random.fold_in(jax.random.fold_in(stream_key, 6), dim), (blocks,), jnp.float32, low / len(cuts), high / len(cuts))
        return jnp.repeat(jnp.exp(steps), dims[dim] // blocks).reshape((-1,) + (1,) * (len(dims) - dim - 1))

    factor_of = one(*cuts[0])
    for cut in cuts[1:]:
        factor_of = factor_of * one(*cut)
    return factor_of


def gaussian(rng, dims, deviation, bound, split=(), dtype=jnp.bfloat16):
    loudness = level_of(rng, dims, split, -0.22, 0.18) if split else 1.0
    result = jax.random.normal(rng, dims, jnp.float32) * deviation * loudness
    return jnp.minimum(jnp.maximum(result, -bound), bound).astype(dtype)


def setup_inputs(seed: int = 0) -> dict:
    streams_of = jax.random.split(jax.random.key(seed), 7)
    tokens = gaussian(streams_of[0], (REPLICAS, TOKENS, D), 1.0, 6.0, ((0, 8), (1, 16)))
    gain = jnp.clip(1.0 + 0.18 * jax.random.normal(streams_of[1], (REPLICAS, D), jnp.float32), 0.1, 1.9)
    next_weights = gaussian(streams_of[2], (REPLICAS, D, KV), D ** -0.5, 0.0625, ((0, 8), (1, 16)))
    weights = gaussian(streams_of[3], (REPLICAS, D, KV), 1.0, 6.0, ((0, 8), (1, 16)))
    snapshot = gaussian(streams_of[4], (D, KV), 1.0, 6.0, ((0, 16),), jnp.float32)
    momentum = gaussian(streams_of[5], (D, KV), 0.5, 3.0, ((0, 16), (1, 8)))
    return {"tokens": tokens, "gain": gain, "next_weights": next_weights, "weights": weights, "snapshot": snapshot, "momentum": momentum}


momentum_decay = 0.9
outer_rate = 0.7

def to_blocks(values, width):
    lead_dims = values.shape[:-1]
    column_count = values.shape[-1]
    grouped = values.reshape(lead_dims + (column_count // width, width))
    largest = lax.optimization_barrier(jnp.max(jnp.abs(grouped), axis=-1))
    target = (largest + 1e-06) / 448.0
    high_part = target.astype(jnp.bfloat16)
    low_part = (target - high_part.astype(jnp.float32)).astype(jnp.bfloat16)
    block_scale = high_part.astype(jnp.float32) + low_part.astype(jnp.float32)
    levels = (grouped / block_scale[..., None]).astype(jnp.bfloat16)
    scales = jnp.stack([high_part, low_part], axis=-1)
    return (levels.reshape(values.shape), scales)

def from_blocks(levels, scales, width):
    lead_dims = levels.shape[:-1]
    column_count = levels.shape[-1]
    grouped = levels.astype(jnp.float32).reshape(lead_dims + (column_count // width, width))
    block_scale = scales[..., 0].astype(jnp.float32) + scales[..., 1].astype(jnp.float32)
    return (grouped * block_scale[..., None]).reshape(levels.shape)

def project(inputs):
    rows_in, gain_row, matrix = inputs
    rows_float = rows_in.astype(jnp.float32)
    square_mean = lax.optimization_barrier(jnp.mean(rows_float * rows_float, axis=1, keepdims=True))
    normed = (rows_float * lax.rsqrt(square_mean + 1e-05) * gain_row[None, :]).astype(jnp.bfloat16)
    return jnp.dot(normed, matrix, preferred_element_type=jnp.float32).astype(jnp.bfloat16)

def reference(tokens, gain, next_weights, weights, snapshot, momentum):
    pseudo_grad = snapshot[None] - weights.astype(jnp.float32)
    levels, scales = to_blocks(pseudo_grad, BLOCK)
    average = lax.optimization_barrier(jnp.sum(from_blocks(levels, scales, BLOCK), axis=0)) / REPLICAS
    new_momentum = (momentum_decay * momentum.astype(jnp.float32) + average).astype(jnp.bfloat16)
    updated = snapshot - outer_rate * (average + momentum_decay * new_momentum.astype(jnp.float32))
    new_levels, new_scales = to_blocks(updated, BLOCK)
    new_weights = from_blocks(new_levels, new_scales, BLOCK).astype(jnp.bfloat16)
    next_keys = lax.map(project, (tokens, gain, next_weights))
    return (next_keys, new_weights, new_momentum)
```

```python
import functools

import jax
import jax.numpy as jnp
from jax import lax
from jax.experimental import pallas as pl
from jax.experimental.pallas import tpu as pltpu
from jax.sharding import PartitionSpec as P

BLOCK = 128
DECAY = 0.9
RATE = 0.7
EPS = 1e-05
MIB = 1024 * 1024

Z, X, C = 4, 2, 2
Y, XL = 4, 2


def fsdp_perm(dz=0, dx=0, dc=0):
    pairs = []
    for z in range(Z):
        for x in range(X):
            for c in range(C):
                to = ((z + dz) % Z) * 4 + ((x + dx) % X) * 2 + (c + dc) % C
                pairs.append((z * 4 + x * 2 + c, to))
    return pairs


def replica_perm(dy=0, dx=0):
    pairs = []
    for y in range(Y):
        for x in range(XL):
            pairs.append((y * XL + x, ((y + dy) % Y) * XL + (x + dx) % XL))
    return pairs


def shift(value, **by):
    return lax.ppermute(value, "fsdp", fsdp_perm(**by))


def shift_replica(value, **by):
    return lax.ppermute(value, "replica", replica_perm(**by))


def cost(flops, nbytes):
    return pl.CostEstimate(flops=flops, bytes_accessed=nbytes, transcendentals=0)


GROUPS = (
    ((0, 0), (3, 0), (1, 0), (0, 1)),
    ((2, 0), (3, 1), (1, 1)),
    ((2, 1),),
)


def group_order(group):
    return [(dz, dx, dc) for dz, dx in group for dc in (0, 1)]


def norm_kernel(width, tokens_ref, gain_ref, *out_refs):
    me = lax.axis_index("fsdp")
    z, x, c = me // 4, (me // 2) % 2, me % 2
    rows, features = tokens_ref.shape[1:]
    total = jnp.zeros((rows, width), jnp.float32)
    for j in range(features // width):
        part = tokens_ref[0, :, j * width : (j + 1) * width].astype(jnp.float32)
        total = total + part * part
    scale = lax.rsqrt(jnp.sum(total, axis=1, keepdims=True) / features + EPS)
    for group, out_ref in zip(GROUPS, out_refs):
        for j, (dz, dx, dc) in enumerate(group_order(group)):
            shard = ((z + dz) % Z) * 4 + ((x + dx) % X) * 2 + (c + dc) % C
            at = pl.ds(pl.multiple_of(shard * width, width), width)
            part = tokens_ref[0, :, at].astype(jnp.float32)
            out_ref[:, j * width : (j + 1) * width] = (
                part * scale * gain_ref[:, at]
            ).astype(jnp.bfloat16)


def norm(tokens, gain, width):
    _, rows, features = tokens.shape
    tile = 64
    widths = [len(group_order(g)) * width for g in GROUPS]
    return pl.pallas_call(
        functools.partial(norm_kernel, width),
        grid=(rows // tile,),
        in_specs=[
            pl.BlockSpec((1, tile, features), lambda i: (0, i, 0)),
            pl.BlockSpec((1, features), lambda i: (0, 0)),
        ],
        out_specs=[pl.BlockSpec((tile, w), lambda i: (i, 0)) for w in widths],
        out_shape=[jax.ShapeDtypeStruct((rows, w), jnp.bfloat16) for w in widths],
        compiler_params=pltpu.CompilerParams(vmem_limit_bytes=24 * MIB),
        cost_estimate=cost(8 * rows * features, 4 * rows * features),
        name="norm",
    )(tokens, gain)


def matmul_kernel(offsets, has_total, *refs):
    normed_ref = refs[0]
    weight_refs = refs[1 : 1 + len(offsets)]
    out_ref = refs[-1]
    total = refs[-2][...] if has_total else None
    for at, weight_ref in zip(offsets, weight_refs):
        depth = weight_ref.shape[0]
        part = jnp.dot(
            normed_ref[:, at : at + depth],
            weight_ref[...],
            preferred_element_type=jnp.float32,
        )
        total = part if total is None else total + part
    out_ref[...] = total.astype(out_ref.dtype).reshape(out_ref.shape)


def matmul(normed, pieces, total, last):
    rows, depth = normed.shape
    columns = pieces[0][1].shape[1]
    tile = 256
    offsets = tuple(at for at, _ in pieces)
    weights = [w for _, w in pieces]
    in_specs = [pl.BlockSpec((rows, depth), lambda n: (0, 0))]
    in_specs += [pl.BlockSpec((w.shape[0], tile), lambda n: (0, n)) for w in weights]
    operands = [normed, *weights]
    if total is not None:
        in_specs.append(pl.BlockSpec((rows, tile), lambda n: (0, n)))
        operands.append(total)
    if last:
        out_spec = pl.BlockSpec((1, rows, tile), lambda n: (0, 0, n))
        out_shape = jax.ShapeDtypeStruct((1, rows, columns), jnp.bfloat16)
    else:
        out_spec = pl.BlockSpec((rows, tile), lambda n: (0, n))
        out_shape = jax.ShapeDtypeStruct((rows, columns), jnp.float32)
    return pl.pallas_call(
        functools.partial(matmul_kernel, offsets, total is not None),
        grid=(columns // tile,),
        in_specs=in_specs,
        out_specs=out_spec,
        out_shape=out_shape,
        compiler_params=pltpu.CompilerParams(vmem_limit_bytes=32 * MIB),
        cost_estimate=cost(2 * rows * depth * columns, 2 * rows * depth + 6 * rows * columns),
        name="project",
    )(*operands)


def scale_of(values):
    target = (jnp.max(jnp.abs(values), axis=1, keepdims=True) + 1e-06) / 448.0
    high = target.astype(jnp.bfloat16).astype(jnp.float32)
    low = (target - high).astype(jnp.bfloat16).astype(jnp.float32)
    return high + low


def rounded(values):
    scale = scale_of(values)
    return (values / scale).astype(jnp.bfloat16).astype(jnp.float32) * scale


def split_kernel(weights_ref, *out_refs):
    y = lax.axis_index("replica") // XL
    width = out_refs[0].shape[1]
    for dy, out_ref in enumerate(out_refs):
        at = pl.multiple_of(((y + dy) % Y) * width, width)
        out_ref[...] = weights_ref[0, :, pl.ds(at, width)]


def partial_kernel(snapshot_ref, *refs):
    weight_refs, (own_ref, other_ref) = refs[:-2], refs[-2:]
    me = lax.axis_index("replica")
    y, x = me // XL, me % XL
    for dx, out_ref in ((0, own_ref), (1, other_ref)):
        column = (x + dx) % XL
        at = pl.multiple_of((y * XL + column) * BLOCK, BLOCK)
        snapshot = snapshot_ref[:, pl.ds(at, BLOCK)]
        inside = pl.ds(pl.multiple_of(column * BLOCK, BLOCK), BLOCK)
        total = None
        for weight_ref in weight_refs:
            part = rounded(snapshot - weight_ref[:, inside].astype(jnp.float32))
            total = part if total is None else total + part
        out_ref[...] = total


def update_kernel(snapshot_ref, momentum_ref, own_ref, other_ref, new_ref, velocity_ref):
    me = lax.axis_index("replica")
    at = pl.multiple_of(me * BLOCK, BLOCK)
    snapshot = snapshot_ref[:, pl.ds(at, BLOCK)]
    average = (own_ref[...] + other_ref[...]) / (Y * XL)
    velocity = (DECAY * momentum_ref[...].astype(jnp.float32) + average).astype(jnp.bfloat16)
    velocity_ref[...] = velocity
    updated = snapshot - RATE * (average + DECAY * velocity.astype(jnp.float32))
    new_ref[...] = rounded(updated).astype(jnp.bfloat16)


def assemble_kernel(*refs):
    piece_refs, out_ref = refs[:-1], refs[-1]
    me = lax.axis_index("replica")
    y, x = me // XL, me % XL
    k = 0
    for dy in range(Y):
        for dx in range(XL):
            owner = ((y + dy) % Y) * XL + (x + dx) % XL
            at = pl.multiple_of(owner * BLOCK, BLOCK)
            out_ref[:, pl.ds(at, BLOCK)] = piece_refs[k][...]
            k += 1


def whole(kernel, out_shape, name, operands):
    spec = pl.BlockSpec(memory_space=pltpu.VMEM)
    nbytes = sum(v.size * v.dtype.itemsize for v in operands)
    return pl.pallas_call(
        kernel,
        in_specs=[spec] * len(operands),
        out_specs=jax.tree.map(lambda _: spec, out_shape),
        out_shape=out_shape,
        compiler_params=pltpu.CompilerParams(vmem_limit_bytes=16 * MIB),
        cost_estimate=cost(8 * nbytes, 2 * nbytes),
        name=name,
    )(*operands)


def body(tokens, gain, next_weights, weights, snapshot, momentum):
    shape = jax.ShapeDtypeStruct
    own = next_weights[0]
    rows, columns = own.shape
    half, quarter = rows // 2, rows // 4

    shards = {(0, 0): own}
    shards[3, 0] = shift(own, dz=1)
    shards[1, 0] = shift(own, dz=-1)
    shards[0, 1] = shift(own, dx=1)

    slices = whole(
        split_kernel,
        [shape((rows, columns // Y), jnp.bfloat16)] * Y,
        "split",
        [weights],
    )
    slices = [slices[0]] + [shift_replica(slices[dy], dy=dy) for dy in range(1, Y)]

    normed = norm(tokens, gain, rows)

    own_sum, other_sum = whole(
        partial_kernel,
        [shape((rows, BLOCK), jnp.float32)] * 2,
        "partial",
        [snapshot, *slices],
    )
    other_sum = shift_replica(other_sum, dx=1)
    new, velocity = whole(
        update_kernel,
        [shape((rows, BLOCK), jnp.bfloat16)] * 2,
        "update",
        [snapshot, momentum, own_sum, other_sum],
    )
    new_other = shift_replica(new, dx=1)
    pieces = []
    for dy in range(Y):
        for value in (new, new_other):
            pieces.append(shift_replica(value, dy=-dy) if dy else value)
    new_weights = whole(
        assemble_kernel, shape((rows, columns), jnp.bfloat16), "assemble", pieces
    )

    def both(value):
        return value, shift(value, dc=1)

    def place(group, *items):
        out = []
        for key, first, pair in items:
            for dc in (0, 1):
                out.append(((group.index(key) * 2 + dc) * rows + first, pair[dc]))
        return out

    first = place(GROUPS[0], *((k, 0, both(shards[k])) for k in GROUPS[0]))

    low_2 = shift(shards[3, 0][:half], dz=1)
    high_2 = shift(shards[1, 0][half:], dz=-1)
    low_31 = shift(shards[0, 1][:half], dz=1)
    low_11 = shift(shards[0, 1][:half], dz=-1)
    high_31 = shift(shards[3, 0][half:], dx=1)
    high_11 = shift(shards[1, 0][half:], dx=1)
    low_21a = shift(low_31[:quarter], dz=1)
    low_21b = shift(low_11[quarter:], dz=-1)
    high_21 = shift(high_2, dx=1)

    second = place(
        GROUPS[1],
        ((2, 0), 0, both(low_2)),
        ((2, 0), half, both(high_2)),
        ((3, 1), 0, both(low_31)),
        ((3, 1), half, both(high_31)),
        ((1, 1), 0, both(low_11)),
        ((1, 1), half, both(high_11)),
    )
    third = place(
        GROUPS[2],
        ((2, 1), 0, both(low_21a)),
        ((2, 1), quarter, both(low_21b)),
        ((2, 1), half, both(high_21)),
    )
    total = matmul(normed[0], first, None, False)
    total = matmul(normed[1], second, total, False)
    next_keys = matmul(normed[2], third, total, True)
    return (next_keys, new_weights, velocity)


def solution(mesh):
    placed = (
        P("replica", "fsdp", None),
        P("replica", None),
        P("replica", "fsdp", None),
        P("replica", "fsdp", None),
        P("fsdp", None),
        P("fsdp", "replica"),
    )
    return jax.shard_map(
        body,
        mesh=mesh,
        in_specs=placed,
        out_specs=(P("replica", "fsdp", None), P("fsdp", None), P("fsdp", "replica")),
        check_vma=False,
    )
```

```python
import functools

import jax
import jax.numpy as jnp
from jax import lax
from jax.experimental import pallas as pl
from jax.experimental.pallas import tpu as pltpu
from jax.sharding import PartitionSpec as P

BLOCK = 128
DECAY = 0.9
RATE = 0.7
EPS = 1e-05
MIB = 1024 * 1024

Z, X, C = 4, 2, 2
Y, XL = 4, 2


def fsdp_perm(move):
    pairs = []
    for z in range(Z):
        for x in range(X):
            for c in range(C):
                to_z, to_x, to_c = move(z, x, c)
                pairs.append((z * 4 + x * 2 + c, (to_z % Z) * 4 + to_x * 2 + to_c))
    return pairs


def along_z(value):
    return lax.ppermute(
        value, "fsdp", fsdp_perm(lambda z, x, c: (z + 1 - 2 * c, x, c))
    )


def along_x(value):
    return lax.ppermute(value, "fsdp", fsdp_perm(lambda z, x, c: (z, 1 - x, c)))


def to_core(value):
    return lax.ppermute(value, "fsdp", fsdp_perm(lambda z, x, c: (z, x, 1 - c)))


def across_replicas(value, move):
    pairs = []
    for y in range(Y):
        for x in range(XL):
            to_y, to_x = move(y, x)
            pairs.append((y * XL + x, (to_y % Y) * XL + to_x))
    return lax.ppermute(value, "replica", pairs)


def cost(flops, nbytes):
    return pl.CostEstimate(flops=flops, bytes_accessed=nbytes, transcendentals=0)


def prepare_kernel(
    gain_hbm, next_hbm, weights_hbm, out_ref, low_ref, high_ref, *refs
):
    slice_refs, (gain_ref, next_ref, sems, slice_sems) = refs[:Y], refs[Y:]
    rows = next_ref.shape[0]
    side = BLOCK
    first = pl.multiple_of(lax.axis_index("fsdp") * rows, rows)
    copies = [
        pltpu.make_async_copy(
            gain_hbm.at[:, pl.ds(first, rows)], gain_ref, sems.at[rows // side]
        )
    ]
    for i in range(rows // side):
        at = slice(i * side, (i + 1) * side)
        copies.append(
            pltpu.make_async_copy(next_hbm.at[0, at, :], next_ref.at[at, :], sems.at[i])
        )
    y = lax.axis_index("replica") // XL
    width = slice_refs[0].shape[1]
    slice_copies = []
    for dy, slice_ref in enumerate(slice_refs):
        at = pl.multiple_of(((y + dy) % Y) * width, width)
        slice_copies.append(
            pltpu.make_async_copy(
                weights_hbm.at[0, :, pl.ds(at, width)], slice_ref, slice_sems.at[dy]
            )
        )
    for copy in copies + slice_copies:
        copy.start()
    eye = lax.broadcasted_iota(jnp.int32, (side, side), 0) == lax.broadcasted_iota(
        jnp.int32, (side, side), 1
    )
    copies[0].wait()
    for i in range(rows // side):
        at = slice(i * side, (i + 1) * side)
        gain = jnp.where(eye, gain_ref[:, at], 0.0)
        column = jnp.sum(gain, axis=1, keepdims=True)
        copies[1 + i].wait()
        block = (next_ref[at, :].astype(jnp.float32) * column).astype(jnp.bfloat16)
        out_ref[at, :] = block
        if i * side < rows // 2:
            low_ref[at, :] = block
        else:
            high_ref[i * side - rows // 2 : (i + 1) * side - rows // 2, :] = block
    for copy in slice_copies:
        copy.wait()


def prepare(gain, next_weights, weights):
    _, rows, columns = next_weights.shape
    hbm = pl.BlockSpec(memory_space=pltpu.HBM)
    shapes = [(rows, columns), (rows // 2, columns), (rows // 2, columns)]
    shapes += [(rows, columns // Y)] * Y
    operands = [gain, next_weights, weights]
    return pl.pallas_call(
        prepare_kernel,
        in_specs=[hbm] * 3,
        out_specs=[pl.BlockSpec(memory_space=pltpu.VMEM)] * len(shapes),
        out_shape=[jax.ShapeDtypeStruct(s, jnp.bfloat16) for s in shapes],
        scratch_shapes=[
            pltpu.VMEM((1, rows), jnp.float32),
            pltpu.VMEM((rows, columns), jnp.bfloat16),
            pltpu.SemaphoreType.DMA((rows // BLOCK + 1,)),
            pltpu.SemaphoreType.DMA((Y,)),
        ],
        compiler_params=pltpu.CompilerParams(vmem_limit_bytes=8 * MIB),
        cost_estimate=cost(rows * columns, 4 * rows * columns),
        name="prepare",
    )(*(pltpu.with_memory_space_constraint(v, pltpu.HBM) for v in operands))


def phase(values, after=()):
    spec = pl.BlockSpec(memory_space=pl.ANY)
    count = len(values)
    return pl.pallas_call(
        lambda *refs: None,
        in_specs=[spec] * (count + len(after)),
        out_specs=[spec] * count,
        out_shape=[jax.ShapeDtypeStruct(v.shape, v.dtype) for v in values],
        input_output_aliases={i: i for i in range(count)},
        compiler_params=pltpu.CompilerParams(vmem_limit_bytes=MIB),
        cost_estimate=cost(0, 0),
        name="phase",
    )(*values, *after)


def half_kernel(tokens_hbm, half_ref, sems):
    shards = sems.shape[0]
    width = half_ref.shape[1] // shards
    other = 1 - lax.axis_index("fsdp") % C
    copies = []
    for k in range(shards):
        at = pl.ds(pl.multiple_of((k * C + other) * width, width), width)
        to = pl.ds(k * width, width)
        copies.append(
            pltpu.make_async_copy(
                tokens_hbm.at[0, :, at], half_ref.at[:, to], sems.at[k]
            )
        )
    for copy in copies:
        copy.start()
    for copy in copies:
        copy.wait()


def load_kernel(tokens_hbm, tokens_ref, scale_ref, sems):
    _, rows, features = tokens_ref.shape
    parts = sems.shape[0]
    size, tile, width = rows // parts, 32, 512

    def copy(i):
        at = pl.ds(pl.multiple_of(i * size, size), size)
        return pltpu.make_async_copy(
            tokens_hbm.at[0, at, :], tokens_ref.at[0, at, :], sems.at[i]
        )

    for i in range(parts):
        copy(i).start()

    def part(i, carry):
        copy(i).wait()
        for k in range(size // tile):
            at = pl.ds(pl.multiple_of(i * size + k * tile, tile), tile)
            total = jnp.zeros((tile, width), jnp.float32)
            for j in range(features // width):
                value = tokens_ref[0, at, j * width : (j + 1) * width]
                value = value.astype(jnp.float32)
                total = total + value * value
            mean = jnp.sum(total, axis=1, keepdims=True) / features
            scale_ref[at, :] = jnp.broadcast_to(lax.rsqrt(mean + EPS), (tile, BLOCK))
        return carry

    lax.fori_loop(0, parts, part, 0)


def fetch(kernel, tokens, out_shapes, copies, name, after):
    spec = pl.BlockSpec(memory_space=pltpu.VMEM)

    def run(tokens_hbm, *refs):
        kernel(tokens_hbm, *refs[len(after) :])

    return pl.pallas_call(
        run,
        in_specs=[pl.BlockSpec(memory_space=pltpu.HBM)]
        + [pl.BlockSpec(memory_space=pl.ANY)] * len(after),
        out_specs=[spec] * len(out_shapes),
        out_shape=out_shapes,
        scratch_shapes=[pltpu.SemaphoreType.DMA((copies,))],
        compiler_params=pltpu.CompilerParams(vmem_limit_bytes=4 * MIB),
        cost_estimate=cost(tokens.size, 2 * tokens.size),
        name=name,
    )(pltpu.with_memory_space_constraint(tokens, pltpu.HBM), *after)


def project_kernel(places, rows, given, *refs):
    count = len(places)
    tokens_ref, half_ref, weight_refs = refs[0], refs[1], refs[2 : 2 + count]
    total_refs = refs[2 + count : 4 + count] if given else None
    out_ref, other_ref = refs[-2:]
    me = lax.axis_index("fsdp")
    z, x, c = me // 4, (me // 2) % 2, me % 2
    starts = []
    for step, dx, dc, first in places:
        block = ((z + (2 * c - 1) * step + Z) % Z) * 2 + (x + dx) % 2
        starts.append(
            (
                pl.multiple_of((block * 2 + c) * rows + first, BLOCK),
                pl.multiple_of(block * rows + first, BLOCK),
            )
        )
    tile = 256

    def column(n, carry):
        at = pl.ds(pl.multiple_of(n * tile, tile), tile)
        total = total_refs[0][:, at] if given else None
        other = total_refs[1][:, at] if given else None
        for (start, half_start), weight_ref in zip(starts, weight_refs):
            depth = weight_ref.shape[0]
            weight = weight_ref[:, at]
            part = jnp.dot(
                tokens_ref[0, :, pl.ds(start, depth)],
                weight,
                preferred_element_type=jnp.float32,
            )
            total = part if total is None else total + part
            part = jnp.dot(
                half_ref[:, pl.ds(half_start, depth)],
                weight,
                preferred_element_type=jnp.float32,
            )
            other = part if other is None else other + part
        out_ref[:, at] = total
        other_ref[:, at] = other.astype(other_ref.dtype)
        return carry

    lax.fori_loop(0, weight_refs[0].shape[1] // tile, column, 0)


def project(tokens, half, pieces, rows, totals=(), after=(), last=False):
    count = tokens.shape[1]
    columns = pieces[0][1].shape[1]
    operands = [tokens, half, *(w for _, w in pieces)]
    aliases = {len(operands) + i: i for i in range(2 - last)} if totals else {}
    operands += totals
    depth = sum(w.shape[0] for _, w in pieces)
    spec = pl.BlockSpec(memory_space=pltpu.VMEM)
    places = tuple(p for p, _ in pieces)
    return pl.pallas_call(
        functools.partial(project_kernel, places, rows, bool(totals)),
        in_specs=[spec] * len(operands)
        + [pl.BlockSpec(memory_space=pl.ANY)] * len(after),
        out_specs=[spec] * 2,
        out_shape=[
            jax.ShapeDtypeStruct((count, columns), jnp.float32),
            jax.ShapeDtypeStruct(
                (count, columns), jnp.bfloat16 if last else jnp.float32
            ),
        ],
        input_output_aliases=aliases,
        compiler_params=pltpu.CompilerParams(vmem_limit_bytes=6 * MIB),
        cost_estimate=cost(4 * count * depth * columns, 2 * columns * depth),
        name="project",
    )(*operands, *after)


def finish_kernel(places, rows, *refs):
    count = len(places)
    tokens_ref, weight_refs = refs[0], refs[1 : 1 + count]
    own_ref, other_ref, scale_ref = refs[1 + count : 4 + count]
    out_ref = refs[-1]
    me = lax.axis_index("fsdp")
    z, x, c = me // 4, (me // 2) % 2, me % 2
    starts = []
    for step, dx, dc, first in places:
        core = (c + dc) % 2
        shard = ((z + (2 * core - 1) * step + Z) % Z) * 4 + ((x + dx) % 2) * 2 + core
        starts.append(pl.multiple_of(shard * rows + first, BLOCK))
    tile = 256

    def column(n, carry):
        at = pl.ds(pl.multiple_of(n * tile, tile), tile)
        total = own_ref[:, at] + other_ref[:, at].astype(jnp.float32)
        for start, weight_ref in zip(starts, weight_refs):
            total = total + jnp.dot(
                tokens_ref[0, :, pl.ds(start, weight_ref.shape[0])],
                weight_ref[:, at],
                preferred_element_type=jnp.float32,
            )
        out_ref[0, :, at] = (total * scale_ref[:, :1]).astype(jnp.bfloat16)
        return carry

    lax.fori_loop(0, weight_refs[0].shape[1] // tile, column, 0)


def finish(tokens, pieces, rows, own, other, row_scale, after):
    count = tokens.shape[1]
    columns = own.shape[1]
    operands = [tokens, *(w for _, w in pieces), own, other, row_scale]
    depth = sum(w.shape[0] for _, w in pieces)
    spec = pl.BlockSpec(memory_space=pltpu.VMEM)
    places = tuple(p for p, _ in pieces)
    return pl.pallas_call(
        functools.partial(finish_kernel, places, rows),
        in_specs=[spec] * len(operands)
        + [pl.BlockSpec(memory_space=pl.ANY)] * len(after),
        out_specs=spec,
        out_shape=jax.ShapeDtypeStruct((1, count, columns), jnp.bfloat16),
        compiler_params=pltpu.CompilerParams(vmem_limit_bytes=6 * MIB),
        cost_estimate=cost(2 * count * depth * columns, 2 * columns * depth),
        name="finish",
    )(*operands, *after)


def scale_of(values):
    target = (jnp.max(jnp.abs(values), axis=1, keepdims=True) + 1e-06) / 448.0
    high = target.astype(jnp.bfloat16).astype(jnp.float32)
    low = (target - high).astype(jnp.bfloat16).astype(jnp.float32)
    return high + low


def rounded(values):
    scale = scale_of(values)
    return (values / scale).astype(jnp.bfloat16).astype(jnp.float32) * scale


def partial_kernel(snapshot_ref, *refs):
    weight_refs, (own_ref, other_ref) = refs[:-2], refs[-2:]
    me = lax.axis_index("replica")
    y, x = me // XL, me % XL
    for dx, out_ref in ((0, own_ref), (1, other_ref)):
        column = (x + dx) % XL
        at = pl.multiple_of((y * XL + column) * BLOCK, BLOCK)
        snapshot = snapshot_ref[:, pl.ds(at, BLOCK)]
        inside = pl.ds(pl.multiple_of(column * BLOCK, BLOCK), BLOCK)
        total = None
        for weight_ref in weight_refs:
            part = rounded(snapshot - weight_ref[:, inside].astype(jnp.float32))
            total = part if total is None else total + part
        out_ref[...] = total.astype(out_ref.dtype)


def update_kernel(snapshot_ref, momentum_ref, own_ref, other_ref, new_ref, velocity_ref):
    me = lax.axis_index("replica")
    at = pl.multiple_of(me * BLOCK, BLOCK)
    snapshot = snapshot_ref[:, pl.ds(at, BLOCK)]
    average = (own_ref[...] + other_ref[...].astype(jnp.float32)) / (Y * XL)
    velocity = (DECAY * momentum_ref[...].astype(jnp.float32) + average).astype(jnp.bfloat16)
    velocity_ref[...] = velocity
    updated = snapshot - RATE * (average + DECAY * velocity.astype(jnp.float32))
    new_ref[...] = rounded(updated).astype(jnp.bfloat16)


def join_kernel(left_ref, right_ref, out_ref):
    width = left_ref.shape[1]
    out_ref[:, :width] = left_ref[...]
    out_ref[:, width:] = right_ref[...]


def join(left, right, after=()):
    rows, columns = left.shape
    out = jax.ShapeDtypeStruct((rows, 2 * columns), left.dtype)
    return whole(join_kernel, out, "join", [left, right], after=after)


def assemble_kernel(*refs):
    pair_refs, (out_ref, done_ref) = refs[:-2], refs[-2:]
    me = lax.axis_index("replica")
    y, x = me // XL, me % XL
    for dy, pair_ref in enumerate(pair_refs):
        for dx in range(XL):
            owner = ((y + dy) % Y) * XL + (x + dx) % XL
            at = pl.multiple_of(owner * BLOCK, BLOCK)
            inside = slice(dx * BLOCK, (dx + 1) * BLOCK)
            out_ref[:, pl.ds(at, BLOCK)] = pair_ref[:, inside]
    done_ref[...] = jnp.zeros_like(done_ref)


def whole(kernel, out_shape, name, operands, after=()):
    spec = pl.BlockSpec(memory_space=pltpu.VMEM)
    nbytes = sum(v.size * v.dtype.itemsize for v in operands)
    count = len(operands)

    def run(*refs):
        kernel(*refs[:count], *refs[count + len(after) :])

    return pl.pallas_call(
        run,
        in_specs=[spec] * count + [pl.BlockSpec(memory_space=pl.ANY)] * len(after),
        out_specs=jax.tree.map(lambda _: spec, out_shape),
        out_shape=out_shape,
        compiler_params=pltpu.CompilerParams(vmem_limit_bytes=4 * MIB),
        cost_estimate=cost(8 * nbytes, 2 * nbytes),
        name=name,
    )(*operands, *after)


def body(tokens, gain, next_weights, weights, snapshot, momentum):
    shape = jax.ShapeDtypeStruct
    _, rows, columns = next_weights.shape
    half = rows // 2

    own, own_low, own_high, *slices = prepare(gain, next_weights, weights)

    ring_1 = along_z(own)
    low_0 = along_x(own_low)
    arrived = [
        across_replicas(slices[dy], lambda y, x, dy=dy: (y + dy, x))
        for dy in range(1, Y)
    ]
    count, features = tokens.shape[1:]
    (half_sent,) = fetch(
        half_kernel,
        tokens,
        [shape((count, features // C), tokens.dtype)],
        Z * X,
        "half",
        [own],
    )
    ring_1, low_0, own_high, half_sent = phase([ring_1, low_0, own_high, half_sent])

    ring_2 = along_z(ring_1)
    high_0 = along_x(own_high)
    tokens_half = to_core(half_sent)
    tokens, row_scale = fetch(
        load_kernel,
        tokens,
        [shape(tokens.shape, tokens.dtype), shape((count, BLOCK), jnp.float32)],
        12,
        "load",
        [ring_1],
    )
    own_sum, other_sum = whole(
        partial_kernel,
        [shape((rows, BLOCK), jnp.float32), shape((rows, BLOCK), jnp.bfloat16)],
        "partial",
        [snapshot, slices[0], *arrived],
        after=[row_scale],
    )
    other_sum = across_replicas(other_sum, lambda y, x: (y, 1 - x))
    ring_2, low_0, high_0, other_sum = phase([ring_2, low_0, high_0, other_sum])

    ring_3 = along_z(ring_2)
    low_1 = along_z(low_0)
    high_2 = along_x(ring_2[half:])
    new, velocity = whole(
        update_kernel,
        [shape((rows, BLOCK), jnp.bfloat16)] * 2,
        "update",
        [snapshot, momentum, own_sum, other_sum],
    )
    new_other = across_replicas(new, lambda y, x: (y, 1 - x))
    totals = project(
        tokens,
        tokens_half,
        [
            ((0, 0, 0, 0), own),
            ((1, 0, 0, 0), ring_1),
            ((2, 0, 0, 0), ring_2),
            ((0, 1, 0, 0), low_0),
            ((0, 1, 0, half), high_0),
        ],
        rows,
        after=[new],
    )
    ring_3, low_1, high_0, high_2, new_other = phase(
        [ring_3, low_1, high_0, high_2, new_other], after=[totals[0]]
    )

    low_2 = along_z(low_1)
    high_1 = along_z(high_0)
    high_3 = along_x(ring_3[half:])
    pair = join(new, new_other)
    pair_1 = across_replicas(pair, lambda y, x: (y - 1, x))
    pair_3 = across_replicas(pair, lambda y, x: (y + 1, x))
    totals = project(
        tokens,
        tokens_half,
        [
            ((3, 0, 0, 0), ring_3),
            ((1, 1, 0, 0), low_1),
            ((2, 1, 0, half), high_2),
        ],
        rows,
        totals,
        after=[pair],
    )
    low_2, high_1, high_3, pair = phase(
        [low_2, high_1, high_3, pair], after=[totals[0], pair_1, pair_3]
    )

    low_3 = along_z(low_2)
    pair_2 = across_replicas(pair, lambda y, x: (y + 2, x))
    own_total, other_total = project(
        tokens,
        tokens_half,
        [
            ((2, 1, 0, 0), low_2),
            ((1, 1, 0, half), high_1),
            ((3, 1, 0, half), high_3),
        ],
        rows,
        totals,
        last=True,
    )
    low_3, pair_2, other_total = phase([low_3, pair_2, other_total])

    low_3_other = to_core(low_3)
    other_total = to_core(other_total)
    new_weights, done = whole(
        assemble_kernel,
        [shape((rows, columns), jnp.bfloat16), shape((8, BLOCK), jnp.float32)],
        "assemble",
        [pair, pair_1, pair_2, pair_3],
    )
    next_keys = finish(
        tokens,
        [((3, 1, 0, 0), low_3), ((3, 1, 1, 0), low_3_other)],
        rows,
        own_total,
        other_total,
        row_scale,
        after=[done],
    )
    return (next_keys, new_weights, velocity)


def solution(mesh):
    placed = (
        P("replica", "fsdp", None),
        P("replica", None),
        P("replica", "fsdp", None),
        P("replica", "fsdp", None),
        P("fsdp", None),
        P("fsdp", "replica"),
    )
    return jax.shard_map(
        body,
        mesh=mesh,
        in_specs=placed,
        out_specs=(P("replica", "fsdp", None), P("fsdp", None), P("fsdp", "replica")),
        check_vma=False,
    )
```

```python
import functools

import jax
import jax.numpy as jnp
from jax import lax
from jax.experimental import pallas as pl
from jax.experimental.pallas import tpu as pltpu
from jax.sharding import PartitionSpec as P

BLOCK = 128
DECAY = 0.9
RATE = 0.7
EPS = 1e-05
MIB = 1024 * 1024

Z, X, C = 4, 2, 2
Y, XL = 4, 2


def fsdp_perm(move):
    pairs = []
    for z in range(Z):
        for x in range(X):
            for c in range(C):
                to_z, to_x, to_c = move(z, x, c)
                pairs.append((z * 4 + x * 2 + c, (to_z % Z) * 4 + to_x * 2 + to_c))
    return pairs


def along_z(value):
    return lax.ppermute(
        value, "fsdp", fsdp_perm(lambda z, x, c: (z + 1 - 2 * c, x, c))
    )


def along_x(value):
    return lax.ppermute(value, "fsdp", fsdp_perm(lambda z, x, c: (z, 1 - x, c)))


def to_core(value):
    return lax.ppermute(value, "fsdp", fsdp_perm(lambda z, x, c: (z, x, 1 - c)))


def across_replicas(value, move):
    pairs = []
    for y in range(Y):
        for x in range(XL):
            to_y, to_x = move(y, x)
            pairs.append((y * XL + x, (to_y % Y) * XL + to_x))
    return lax.ppermute(value, "replica", pairs)


def cost(flops, nbytes):
    return pl.CostEstimate(flops=flops, bytes_accessed=nbytes, transcendentals=0)


def prepare_kernel(
    gain_hbm, next_hbm, weights_hbm, out_ref, low_ref, high_ref, *refs
):
    slice_refs, (gain_ref, next_ref, sems, slice_sems) = refs[:Y], refs[Y:]
    rows = next_ref.shape[0]
    side = BLOCK
    first = pl.multiple_of(lax.axis_index("fsdp") * rows, rows)
    copies = [
        pltpu.make_async_copy(
            gain_hbm.at[:, pl.ds(first, rows)], gain_ref, sems.at[rows // side]
        )
    ]
    for i in range(rows // side):
        at = slice(i * side, (i + 1) * side)
        copies.append(
            pltpu.make_async_copy(next_hbm.at[0, at, :], next_ref.at[at, :], sems.at[i])
        )
    y = lax.axis_index("replica") // XL
    width = slice_refs[0].shape[1]
    slice_copies = []
    for dy, slice_ref in enumerate(slice_refs):
        at = pl.multiple_of(((y + dy) % Y) * width, width)
        slice_copies.append(
            pltpu.make_async_copy(
                weights_hbm.at[0, :, pl.ds(at, width)], slice_ref, slice_sems.at[dy]
            )
        )
    for copy in copies + slice_copies:
        copy.start()
    eye = lax.broadcasted_iota(jnp.int32, (side, side), 0) == lax.broadcasted_iota(
        jnp.int32, (side, side), 1
    )
    copies[0].wait()
    for i in range(rows // side):
        at = slice(i * side, (i + 1) * side)
        gain = jnp.where(eye, gain_ref[:, at], 0.0)
        column = jnp.sum(gain, axis=1, keepdims=True)
        copies[1 + i].wait()
        block = (next_ref[at, :].astype(jnp.float32) * column).astype(jnp.bfloat16)
        out_ref[at, :] = block
        if i * side < rows // 2:
            low_ref[at, :] = block
        else:
            high_ref[i * side - rows // 2 : (i + 1) * side - rows // 2, :] = block
    for copy in slice_copies:
        copy.wait()


def prepare(gain, next_weights, weights):
    _, rows, columns = next_weights.shape
    hbm = pl.BlockSpec(memory_space=pltpu.HBM)
    shapes = [(rows, columns), (rows // 2, columns), (rows // 2, columns)]
    shapes += [(rows, columns // Y)] * Y
    operands = [gain, next_weights, weights]
    return pl.pallas_call(
        prepare_kernel,
        in_specs=[hbm] * 3,
        out_specs=[pl.BlockSpec(memory_space=pltpu.VMEM)] * len(shapes),
        out_shape=[jax.ShapeDtypeStruct(s, jnp.bfloat16) for s in shapes],
        scratch_shapes=[
            pltpu.VMEM((1, rows), jnp.float32),
            pltpu.VMEM((rows, columns), jnp.bfloat16),
            pltpu.SemaphoreType.DMA((rows // BLOCK + 1,)),
            pltpu.SemaphoreType.DMA((Y,)),
        ],
        compiler_params=pltpu.CompilerParams(vmem_limit_bytes=8 * MIB),
        cost_estimate=cost(rows * columns, 4 * rows * columns),
        name="prepare",
    )(*(pltpu.with_memory_space_constraint(v, pltpu.HBM) for v in operands))


def phase(values, after=()):
    spec = pl.BlockSpec(memory_space=pl.ANY)
    count = len(values)
    return pl.pallas_call(
        lambda *refs: None,
        in_specs=[spec] * (count + len(after)),
        out_specs=[spec] * count,
        out_shape=[jax.ShapeDtypeStruct(v.shape, v.dtype) for v in values],
        input_output_aliases={i: i for i in range(count)},
        compiler_params=pltpu.CompilerParams(vmem_limit_bytes=MIB),
        cost_estimate=cost(0, 0),
        name="phase",
    )(*values, *after)


def load_kernel(tokens_hbm, tokens_ref, scale_ref, sems):
    _, rows, features = tokens_ref.shape
    parts = sems.shape[0]
    size, tile, width = rows // parts, 32, 512

    def copy(i):
        at = pl.ds(pl.multiple_of(i * size, size), size)
        return pltpu.make_async_copy(
            tokens_hbm.at[0, at, :], tokens_ref.at[0, at, :], sems.at[i]
        )

    for i in range(parts):
        copy(i).start()

    def part(i, carry):
        copy(i).wait()
        for k in range(size // tile):
            at = pl.ds(pl.multiple_of(i * size + k * tile, tile), tile)
            total = jnp.zeros((tile, width), jnp.float32)
            for j in range(features // width):
                value = tokens_ref[0, at, j * width : (j + 1) * width]
                value = value.astype(jnp.float32)
                total = total + value * value
            mean = jnp.sum(total, axis=1, keepdims=True) / features
            scale_ref[at, :] = jnp.broadcast_to(lax.rsqrt(mean + EPS), (tile, BLOCK))
        return carry

    lax.fori_loop(0, parts, part, 0)


def fetch(kernel, tokens, out_shapes, copies, name, after):
    spec = pl.BlockSpec(memory_space=pltpu.VMEM)

    def run(tokens_hbm, *refs):
        kernel(tokens_hbm, *refs[len(after) :])

    return pl.pallas_call(
        run,
        in_specs=[pl.BlockSpec(memory_space=pltpu.HBM)]
        + [pl.BlockSpec(memory_space=pl.ANY)] * len(after),
        out_specs=[spec] * len(out_shapes),
        out_shape=out_shapes,
        scratch_shapes=[pltpu.SemaphoreType.DMA((copies,))],
        compiler_params=pltpu.CompilerParams(vmem_limit_bytes=4 * MIB),
        cost_estimate=cost(tokens.size, 2 * tokens.size),
        name=name,
    )(pltpu.with_memory_space_constraint(tokens, pltpu.HBM), *after)


def project_kernel(places, rows, given, *refs):
    count = len(places)
    tokens_ref, other_tokens_ref, weight_refs = refs[0], refs[1], refs[2 : 2 + count]
    total_refs = refs[2 + count : 4 + count] if given else None
    out_ref, other_ref = refs[-2:]
    me = lax.axis_index("fsdp")
    z, x, c = me // 4, (me // 2) % 2, me % 2
    starts = []
    for step, dx, dc, first in places:
        block = ((z + (2 * c - 1) * step + Z) % Z) * 2 + (x + dx) % 2
        starts.append(pl.multiple_of((block * 2 + c) * rows + first, BLOCK))
    tile = 256

    def column(n, carry):
        at = pl.ds(pl.multiple_of(n * tile, tile), tile)
        total = total_refs[0][:, at] if given else None
        other = total_refs[1][:, at] if given else None
        for start, weight_ref in zip(starts, weight_refs):
            depth = weight_ref.shape[0]
            weight = weight_ref[:, at]
            part = jnp.dot(
                tokens_ref[0, :, pl.ds(start, depth)],
                weight,
                preferred_element_type=jnp.float32,
            )
            total = part if total is None else total + part
            part = jnp.dot(
                other_tokens_ref[0, :, pl.ds(start, depth)],
                weight,
                preferred_element_type=jnp.float32,
            )
            other = part if other is None else other + part
        out_ref[:, at] = total
        other_ref[:, at] = other.astype(other_ref.dtype)
        return carry

    lax.fori_loop(0, weight_refs[0].shape[1] // tile, column, 0)


def project(tokens, other_tokens, pieces, rows, totals=(), after=(), last=False):
    count = tokens.shape[1]
    columns = pieces[0][1].shape[1]
    operands = [tokens, other_tokens, *(w for _, w in pieces)]
    aliases = {len(operands) + i: i for i in range(2 - last)} if totals else {}
    operands += totals
    depth = sum(w.shape[0] for _, w in pieces)
    spec = pl.BlockSpec(memory_space=pltpu.VMEM)
    places = tuple(p for p, _ in pieces)
    return pl.pallas_call(
        functools.partial(project_kernel, places, rows, bool(totals)),
        in_specs=[spec] * len(operands)
        + [pl.BlockSpec(memory_space=pl.ANY)] * len(after),
        out_specs=[spec] * 2,
        out_shape=[
            jax.ShapeDtypeStruct((count, columns), jnp.float32),
            jax.ShapeDtypeStruct(
                (count, columns), jnp.bfloat16 if last else jnp.float32
            ),
        ],
        input_output_aliases=aliases,
        compiler_params=pltpu.CompilerParams(vmem_limit_bytes=6 * MIB),
        cost_estimate=cost(4 * count * depth * columns, 2 * columns * depth),
        name="project",
    )(*operands, *after)


def finish_kernel(places, rows, *refs):
    count = len(places)
    tokens_ref, weight_refs = refs[0], refs[1 : 1 + count]
    own_ref, other_ref, scale_ref = refs[1 + count : 4 + count]
    out_ref = refs[-1]
    me = lax.axis_index("fsdp")
    z, x, c = me // 4, (me // 2) % 2, me % 2
    starts = []
    for step, dx, dc, first in places:
        core = (c + dc) % 2
        shard = ((z + (2 * core - 1) * step + Z) % Z) * 4 + ((x + dx) % 2) * 2 + core
        starts.append(pl.multiple_of(shard * rows + first, BLOCK))
    tile = 256

    def column(n, carry):
        at = pl.ds(pl.multiple_of(n * tile, tile), tile)
        total = own_ref[:, at] + other_ref[:, at].astype(jnp.float32)
        for start, weight_ref in zip(starts, weight_refs):
            total = total + jnp.dot(
                tokens_ref[0, :, pl.ds(start, weight_ref.shape[0])],
                weight_ref[:, at],
                preferred_element_type=jnp.float32,
            )
        out_ref[0, :, at] = (total * scale_ref[:, :1]).astype(jnp.bfloat16)
        return carry

    lax.fori_loop(0, weight_refs[0].shape[1] // tile, column, 0)


def finish(tokens, pieces, rows, own, other, row_scale, after):
    count = tokens.shape[1]
    columns = own.shape[1]
    operands = [tokens, *(w for _, w in pieces), own, other, row_scale]
    depth = sum(w.shape[0] for _, w in pieces)
    spec = pl.BlockSpec(memory_space=pltpu.VMEM)
    places = tuple(p for p, _ in pieces)
    return pl.pallas_call(
        functools.partial(finish_kernel, places, rows),
        in_specs=[spec] * len(operands)
        + [pl.BlockSpec(memory_space=pl.ANY)] * len(after),
        out_specs=spec,
        out_shape=jax.ShapeDtypeStruct((1, count, columns), jnp.bfloat16),
        compiler_params=pltpu.CompilerParams(vmem_limit_bytes=6 * MIB),
        cost_estimate=cost(2 * count * depth * columns, 2 * columns * depth),
        name="finish",
    )(*operands, *after)


def scale_of(values):
    target = (jnp.max(jnp.abs(values), axis=1, keepdims=True) + 1e-06) / 448.0
    high = target.astype(jnp.bfloat16).astype(jnp.float32)
    low = (target - high).astype(jnp.bfloat16).astype(jnp.float32)
    return high + low


def rounded(values):
    scale = scale_of(values)
    return (values / scale).astype(jnp.bfloat16).astype(jnp.float32) * scale


def partial_kernel(snapshot_ref, *refs):
    weight_refs, (own_ref, other_ref) = refs[:-2], refs[-2:]
    me = lax.axis_index("replica")
    y, x = me // XL, me % XL
    for dx, out_ref in ((0, own_ref), (1, other_ref)):
        column = (x + dx) % XL
        at = pl.multiple_of((y * XL + column) * BLOCK, BLOCK)
        snapshot = snapshot_ref[:, pl.ds(at, BLOCK)]
        inside = pl.ds(pl.multiple_of(column * BLOCK, BLOCK), BLOCK)
        total = None
        for weight_ref in weight_refs:
            part = rounded(snapshot - weight_ref[:, inside].astype(jnp.float32))
            total = part if total is None else total + part
        out_ref[...] = total.astype(out_ref.dtype)


def update_kernel(snapshot_ref, momentum_ref, own_ref, other_ref, new_ref, velocity_ref):
    me = lax.axis_index("replica")
    at = pl.multiple_of(me * BLOCK, BLOCK)
    snapshot = snapshot_ref[:, pl.ds(at, BLOCK)]
    average = (own_ref[...] + other_ref[...].astype(jnp.float32)) / (Y * XL)
    velocity = (DECAY * momentum_ref[...].astype(jnp.float32) + average).astype(jnp.bfloat16)
    velocity_ref[...] = velocity
    updated = snapshot - RATE * (average + DECAY * velocity.astype(jnp.float32))
    new_ref[...] = rounded(updated).astype(jnp.bfloat16)


def join_kernel(left_ref, right_ref, out_ref):
    width = left_ref.shape[1]
    out_ref[:, :width] = left_ref[...]
    out_ref[:, width:] = right_ref[...]


def join(left, right, after=()):
    rows, columns = left.shape
    out = jax.ShapeDtypeStruct((rows, 2 * columns), left.dtype)
    return whole(join_kernel, out, "join", [left, right], after=after)


def assemble_kernel(*refs):
    pair_refs, (out_ref, done_ref) = refs[:-2], refs[-2:]
    me = lax.axis_index("replica")
    y, x = me // XL, me % XL
    for dy, pair_ref in enumerate(pair_refs):
        for dx in range(XL):
            owner = ((y + dy) % Y) * XL + (x + dx) % XL
            at = pl.multiple_of(owner * BLOCK, BLOCK)
            inside = slice(dx * BLOCK, (dx + 1) * BLOCK)
            out_ref[:, pl.ds(at, BLOCK)] = pair_ref[:, inside]
    done_ref[...] = jnp.zeros_like(done_ref)


def whole(kernel, out_shape, name, operands, after=()):
    spec = pl.BlockSpec(memory_space=pltpu.VMEM)
    nbytes = sum(v.size * v.dtype.itemsize for v in operands)
    count = len(operands)

    def run(*refs):
        kernel(*refs[:count], *refs[count + len(after) :])

    return pl.pallas_call(
        run,
        in_specs=[spec] * count + [pl.BlockSpec(memory_space=pl.ANY)] * len(after),
        out_specs=jax.tree.map(lambda _: spec, out_shape),
        out_shape=out_shape,
        compiler_params=pltpu.CompilerParams(vmem_limit_bytes=4 * MIB),
        cost_estimate=cost(8 * nbytes, 2 * nbytes),
        name=name,
    )(*operands, *after)


def body(tokens, gain, next_weights, weights, snapshot, momentum):
    shape = jax.ShapeDtypeStruct
    _, rows, columns = next_weights.shape
    half = rows // 2

    own, own_low, own_high, *slices = prepare(gain, next_weights, weights)

    def project_on(totals, pieces, after=(), last=False):
        return project(tokens, other_tokens, pieces, rows, totals, after, last)

    other_tokens = to_core(tokens)
    ring_1 = along_z(own)
    low_0 = along_x(own_low)
    arrived_1 = across_replicas(slices[1], lambda y, x: (y + 1, x))
    arrived_3 = across_replicas(slices[3], lambda y, x: (y - 1, x))
    tokens, row_scale = fetch(
        load_kernel,
        tokens,
        [shape(tokens.shape, tokens.dtype), shape((tokens.shape[1], BLOCK), jnp.float32)],
        12,
        "load",
        [own],
    )
    ring_1, low_0, own_high, slice_2 = phase(
        [ring_1, low_0, own_high, slices[2]], after=[row_scale, arrived_1, arrived_3]
    )

    ring_2 = along_z(ring_1)
    high_0 = along_x(own_high)
    low_1 = along_z(low_0)
    arrived_2 = across_replicas(slice_2, lambda y, x: (y + 2, x))
    totals = project_on((), [((0, 0, 0, 0), own), ((1, 0, 0, 0), ring_1)])
    own_sum, other_sum = whole(
        partial_kernel,
        [shape((rows, BLOCK), jnp.float32), shape((rows, BLOCK), jnp.bfloat16)],
        "partial",
        [snapshot, slices[0], arrived_1, arrived_2, arrived_3],
        after=[totals[0]],
    )
    other_sum = across_replicas(other_sum, lambda y, x: (y, 1 - x))
    ring_2, high_0, low_1, other_sum = phase([ring_2, high_0, low_1, other_sum])

    ring_3 = along_z(ring_2)
    low_2 = along_z(low_1)
    new, velocity = whole(
        update_kernel,
        [shape((rows, BLOCK), jnp.bfloat16)] * 2,
        "update",
        [snapshot, momentum, own_sum, other_sum],
    )
    new_other = across_replicas(new, lambda y, x: (y, 1 - x))
    (high_2,) = phase([ring_2[half:]], after=[new_other])
    high_2 = along_x(high_2)
    pair = join(new, new_other)
    pair_1 = across_replicas(pair, lambda y, x: (y - 1, x))
    pair_3 = across_replicas(pair, lambda y, x: (y + 1, x))
    totals = project_on(
        totals,
        [
            ((2, 0, 0, 0), ring_2),
            ((0, 1, 0, 0), low_0),
            ((0, 1, 0, half), high_0),
        ],
        after=[pair],
    )
    ring_3, high_0, pair = phase(
        [ring_3, high_0, pair], after=[totals[0], pair_1, pair_3]
    )

    high_1 = along_z(high_0)
    high_3 = along_x(ring_3[half:])
    pair_2 = across_replicas(pair, lambda y, x: (y + 2, x))
    totals = project_on(
        totals,
        [
            ((3, 0, 0, 0), ring_3),
            ((1, 1, 0, 0), low_1),
        ],
    )
    (low_2,) = phase([low_2], after=[totals[0]])

    low_3 = along_z(low_2)
    own_total, other_total = project_on(
        totals,
        [
            ((2, 1, 0, half), high_2),
            ((2, 1, 0, 0), low_2),
            ((1, 1, 0, half), high_1),
        ],
        last=True,
    )
    low_3, high_3, pair_2, other_total = phase([low_3, high_3, pair_2, other_total])

    low_3_other, high_3_other = to_core(low_3), to_core(high_3)
    other_total = to_core(other_total)
    new_weights, done = whole(
        assemble_kernel,
        [shape((rows, columns), jnp.bfloat16), shape((8, BLOCK), jnp.float32)],
        "assemble",
        [pair, pair_1, pair_2, pair_3],
    )
    next_keys = finish(
        tokens,
        [
            ((3, 1, 0, 0), low_3),
            ((3, 1, 0, half), high_3),
            ((3, 1, 1, 0), low_3_other),
            ((3, 1, 1, half), high_3_other),
        ],
        rows,
        own_total,
        other_total,
        row_scale,
        after=[done],
    )
    return (next_keys, new_weights, velocity)


def solution(mesh):
    placed = (
        P("replica", "fsdp", None),
        P("replica", None),
        P("replica", "fsdp", None),
        P("replica", "fsdp", None),
        P("fsdp", None),
        P("fsdp", "replica"),
    )
    return jax.shard_map(
        body,
        mesh=mesh,
        in_specs=placed,
        out_specs=(P("replica", "fsdp", None), P("fsdp", None), P("fsdp", "replica")),
        check_vma=False,
    )
```

```python
import functools

import jax
import jax.numpy as jnp
from jax import lax
from jax.experimental import pallas as pl
from jax.experimental.pallas import tpu as pltpu
from jax.sharding import PartitionSpec as P

BLOCK = 128
DECAY = 0.9
RATE = 0.7
EPS = 1e-05
MIB = 1024 * 1024

Z, X, C = 4, 2, 2
Y, XL = 4, 2


def fsdp_perm(move):
    pairs = []
    for z in range(Z):
        for x in range(X):
            for c in range(C):
                to_z, to_x, to_c = move(z, x, c)
                pairs.append((z * 4 + x * 2 + c, (to_z % Z) * 4 + to_x * 2 + to_c))
    return pairs


def along_z(value):
    return lax.ppermute(
        value, "fsdp", fsdp_perm(lambda z, x, c: (z + 1 - 2 * c, x, c))
    )


def along_x(value):
    return lax.ppermute(value, "fsdp", fsdp_perm(lambda z, x, c: (z, 1 - x, c)))


def to_core(value):
    return lax.ppermute(value, "fsdp", fsdp_perm(lambda z, x, c: (z, x, 1 - c)))


def across_replicas(value, move):
    pairs = []
    for y in range(Y):
        for x in range(XL):
            to_y, to_x = move(y, x)
            pairs.append((y * XL + x, (to_y % Y) * XL + to_x))
    return lax.ppermute(value, "replica", pairs)


def cost(flops, nbytes):
    return pl.CostEstimate(flops=flops, bytes_accessed=nbytes, transcendentals=0)


def prepare_kernel(
    gain_hbm, next_hbm, weights_hbm, out_ref, low_ref, high_ref, *refs
):
    slice_refs, (gain_ref, next_ref, sems, slice_sems) = refs[:Y], refs[Y:]
    rows = next_ref.shape[0]
    side = BLOCK
    first = pl.multiple_of(lax.axis_index("fsdp") * rows, rows)
    copies = [
        pltpu.make_async_copy(
            gain_hbm.at[:, pl.ds(first, rows)], gain_ref, sems.at[rows // side]
        )
    ]
    for i in range(rows // side):
        at = slice(i * side, (i + 1) * side)
        copies.append(
            pltpu.make_async_copy(next_hbm.at[0, at, :], next_ref.at[at, :], sems.at[i])
        )
    y = lax.axis_index("replica") // XL
    width = slice_refs[0].shape[1]
    slice_copies = []
    for dy, slice_ref in enumerate(slice_refs):
        at = pl.multiple_of(((y + dy) % Y) * width, width)
        slice_copies.append(
            pltpu.make_async_copy(
                weights_hbm.at[0, :, pl.ds(at, width)], slice_ref, slice_sems.at[dy]
            )
        )
    for copy in copies + slice_copies:
        copy.start()
    eye = lax.broadcasted_iota(jnp.int32, (side, side), 0) == lax.broadcasted_iota(
        jnp.int32, (side, side), 1
    )
    copies[0].wait()
    for i in range(rows // side):
        at = slice(i * side, (i + 1) * side)
        gain = jnp.where(eye, gain_ref[:, at], 0.0)
        column = jnp.sum(gain, axis=1, keepdims=True)
        copies[1 + i].wait()
        block = (next_ref[at, :].astype(jnp.float32) * column).astype(jnp.bfloat16)
        out_ref[at, :] = block
        if i * side < rows // 2:
            low_ref[at, :] = block
        else:
            high_ref[i * side - rows // 2 : (i + 1) * side - rows // 2, :] = block
    for copy in slice_copies:
        copy.wait()


def prepare(gain, next_weights, weights):
    _, rows, columns = next_weights.shape
    hbm = pl.BlockSpec(memory_space=pltpu.HBM)
    shapes = [(rows, columns), (rows // 2, columns), (rows // 2, columns)]
    shapes += [(rows, columns // Y)] * Y
    operands = [gain, next_weights, weights]
    return pl.pallas_call(
        prepare_kernel,
        in_specs=[hbm] * 3,
        out_specs=[pl.BlockSpec(memory_space=pltpu.VMEM)] * len(shapes),
        out_shape=[jax.ShapeDtypeStruct(s, jnp.bfloat16) for s in shapes],
        scratch_shapes=[
            pltpu.VMEM((1, rows), jnp.float32),
            pltpu.VMEM((rows, columns), jnp.bfloat16),
            pltpu.SemaphoreType.DMA((rows // BLOCK + 1,)),
            pltpu.SemaphoreType.DMA((Y,)),
        ],
        compiler_params=pltpu.CompilerParams(vmem_limit_bytes=8 * MIB),
        cost_estimate=cost(rows * columns, 4 * rows * columns),
        name="prepare",
    )(*(pltpu.with_memory_space_constraint(v, pltpu.HBM) for v in operands))


def phase(values, after=()):
    spec = pl.BlockSpec(memory_space=pl.ANY)
    count = len(values)
    return pl.pallas_call(
        lambda *refs: None,
        in_specs=[spec] * (count + len(after)),
        out_specs=[spec] * count,
        out_shape=[jax.ShapeDtypeStruct(v.shape, v.dtype) for v in values],
        input_output_aliases={i: i for i in range(count)},
        compiler_params=pltpu.CompilerParams(vmem_limit_bytes=MIB),
        cost_estimate=cost(0, 0),
        name="phase",
    )(*values, *after)


def load_kernel(tokens_hbm, tokens_ref, scale_ref, sems):
    _, rows, features = tokens_ref.shape
    parts = sems.shape[0]
    size, tile, width = rows // parts, 32, 512

    def copy(i):
        at = pl.ds(pl.multiple_of(i * size, size), size)
        return pltpu.make_async_copy(
            tokens_hbm.at[0, at, :], tokens_ref.at[0, at, :], sems.at[i]
        )

    for i in range(parts):
        copy(i).start()

    def part(i, carry):
        copy(i).wait()
        for k in range(size // tile):
            at = pl.ds(pl.multiple_of(i * size + k * tile, tile), tile)
            total = jnp.zeros((tile, width), jnp.float32)
            for j in range(features // width):
                value = tokens_ref[0, at, j * width : (j + 1) * width]
                value = value.astype(jnp.float32)
                total = total + value * value
            mean = jnp.sum(total, axis=1, keepdims=True) / features
            scale_ref[at, :] = jnp.broadcast_to(lax.rsqrt(mean + EPS), (tile, BLOCK))
        return carry

    lax.fori_loop(0, parts, part, 0)


def fetch(kernel, tokens, out_shapes, copies, name, after):
    spec = pl.BlockSpec(memory_space=pltpu.VMEM)

    def run(tokens_hbm, *refs):
        kernel(tokens_hbm, *refs[len(after) :])

    return pl.pallas_call(
        run,
        in_specs=[pl.BlockSpec(memory_space=pltpu.HBM)]
        + [pl.BlockSpec(memory_space=pl.ANY)] * len(after),
        out_specs=[spec] * len(out_shapes),
        out_shape=out_shapes,
        scratch_shapes=[pltpu.SemaphoreType.DMA((copies,))],
        compiler_params=pltpu.CompilerParams(vmem_limit_bytes=4 * MIB),
        cost_estimate=cost(tokens.size, 2 * tokens.size),
        name=name,
    )(pltpu.with_memory_space_constraint(tokens, pltpu.HBM), *after)


def project_kernel(places, rows, given, *refs):
    count = len(places)
    tokens_ref, other_tokens_ref, weight_refs = refs[0], refs[1], refs[2 : 2 + count]
    total_refs = refs[2 + count : 4 + count] if given else None
    out_ref, other_ref = refs[-2:]
    me = lax.axis_index("fsdp")
    z, x, c = me // 4, (me // 2) % 2, me % 2
    starts = []
    for step, dx, dc, first in places:
        block = ((z + (2 * c - 1) * step + Z) % Z) * 2 + (x + dx) % 2
        starts.append(pl.multiple_of((block * 2 + c) * rows + first, BLOCK))
    tile = 256

    def column(n, carry):
        at = pl.ds(pl.multiple_of(n * tile, tile), tile)
        total = total_refs[0][:, at] if given else None
        other = total_refs[1][:, at] if given else None
        for start, weight_ref in zip(starts, weight_refs):
            depth = weight_ref.shape[0]
            weight = weight_ref[:, at]
            part = jnp.dot(
                tokens_ref[0, :, pl.ds(start, depth)],
                weight,
                preferred_element_type=jnp.float32,
            )
            total = part if total is None else total + part
            part = jnp.dot(
                other_tokens_ref[0, :, pl.ds(start, depth)],
                weight,
                preferred_element_type=jnp.float32,
            )
            other = part if other is None else other + part
        out_ref[:, at] = total
        other_ref[:, at] = other.astype(other_ref.dtype)
        return carry

    lax.fori_loop(0, weight_refs[0].shape[1] // tile, column, 0)


def project(tokens, other_tokens, pieces, rows, totals=(), after=(), last=False, counted=True):
    count = tokens.shape[1]
    columns = pieces[0][1].shape[1]
    operands = [tokens, other_tokens, *(w for _, w in pieces)]
    aliases = {len(operands) + i: i for i in range(2 - last)} if totals else {}
    operands += totals
    depth = sum(w.shape[0] for _, w in pieces)
    spec = pl.BlockSpec(memory_space=pltpu.VMEM)
    places = tuple(p for p, _ in pieces)
    return pl.pallas_call(
        functools.partial(project_kernel, places, rows, bool(totals)),
        in_specs=[spec] * len(operands)
        + [pl.BlockSpec(memory_space=pl.ANY)] * len(after),
        out_specs=[spec] * 2,
        out_shape=[
            jax.ShapeDtypeStruct((count, columns), jnp.float32),
            jax.ShapeDtypeStruct(
                (count, columns), jnp.bfloat16 if last else jnp.float32
            ),
        ],
        input_output_aliases=aliases,
        compiler_params=pltpu.CompilerParams(vmem_limit_bytes=6 * MIB),
        cost_estimate=cost(4 * count * depth * columns, 2 * columns * depth)
        if counted
        else cost(1, 1),
        name="project",
    )(*operands, *after)


def finish_kernel(places, rows, given, last, *refs):
    count = len(places)
    tokens_ref, weight_refs = refs[0], refs[1 : 1 + count]
    total_refs = refs[1 + count : 1 + count + given]
    out_ref = refs[-1]
    me = lax.axis_index("fsdp")
    z, x, c = me // 4, (me // 2) % 2, me % 2
    starts = []
    for step, dx, dc, first in places:
        core = (c + dc) % 2
        shard = ((z + (2 * core - 1) * step + Z) % Z) * 4 + ((x + dx) % 2) * 2 + core
        starts.append(pl.multiple_of(shard * rows + first, BLOCK))
    tile = 256

    def column(n, carry):
        at = pl.ds(pl.multiple_of(n * tile, tile), tile)
        total = total_refs[0][:, at]
        for total_ref in total_refs[1:]:
            total = total + total_ref[:, at].astype(jnp.float32)
        for start, weight_ref in zip(starts, weight_refs):
            total = total + jnp.dot(
                tokens_ref[0, :, pl.ds(start, weight_ref.shape[0])],
                weight_ref[:, at],
                preferred_element_type=jnp.float32,
            )
        if last:
            scale_ref = refs[1 + count + given]
            out_ref[0, :, at] = (total * scale_ref[:, :1]).astype(jnp.bfloat16)
        else:
            out_ref[:, at] = total
        return carry

    lax.fori_loop(0, weight_refs[0].shape[1] // tile, column, 0)


def finish(tokens, pieces, rows, totals, row_scale=None, after=()):
    count = tokens.shape[1]
    columns = totals[0].shape[1]
    last = row_scale is not None
    operands = [tokens, *(w for _, w in pieces), *totals]
    if last:
        operands.append(row_scale)
        out_shape = jax.ShapeDtypeStruct((1, count, columns), jnp.bfloat16)
    else:
        out_shape = jax.ShapeDtypeStruct((count, columns), jnp.float32)
    depth = sum(w.shape[0] for _, w in pieces)
    spec = pl.BlockSpec(memory_space=pltpu.VMEM)
    places = tuple(p for p, _ in pieces)
    return pl.pallas_call(
        functools.partial(finish_kernel, places, rows, len(totals), last),
        in_specs=[spec] * len(operands)
        + [pl.BlockSpec(memory_space=pl.ANY)] * len(after),
        out_specs=spec,
        out_shape=out_shape,
        input_output_aliases={} if last else {1 + len(pieces): 0},
        compiler_params=pltpu.CompilerParams(vmem_limit_bytes=6 * MIB),
        cost_estimate=cost(2 * count * depth * columns, 2 * columns * depth),
        name="finish",
    )(*operands, *after)


def scale_of(values):
    target = (jnp.max(jnp.abs(values), axis=1, keepdims=True) + 1e-06) / 448.0
    high = target.astype(jnp.bfloat16).astype(jnp.float32)
    low = (target - high).astype(jnp.bfloat16).astype(jnp.float32)
    return high + low


def rounded(values):
    scale = scale_of(values)
    return (values / scale).astype(jnp.bfloat16).astype(jnp.float32) * scale


def partial_kernel(snapshot_ref, *refs):
    weight_refs, (own_ref, other_ref) = refs[:-2], refs[-2:]
    me = lax.axis_index("replica")
    y, x = me // XL, me % XL
    for dx, out_ref in ((0, own_ref), (1, other_ref)):
        column = (x + dx) % XL
        at = pl.multiple_of((y * XL + column) * BLOCK, BLOCK)
        snapshot = snapshot_ref[:, pl.ds(at, BLOCK)]
        inside = pl.ds(pl.multiple_of(column * BLOCK, BLOCK), BLOCK)
        total = None
        for weight_ref in weight_refs:
            part = rounded(snapshot - weight_ref[:, inside].astype(jnp.float32))
            total = part if total is None else total + part
        out_ref[...] = total.astype(out_ref.dtype)


def update_kernel(snapshot_ref, momentum_ref, own_ref, other_ref, new_ref, velocity_ref):
    me = lax.axis_index("replica")
    at = pl.multiple_of(me * BLOCK, BLOCK)
    snapshot = snapshot_ref[:, pl.ds(at, BLOCK)]
    average = (own_ref[...] + other_ref[...].astype(jnp.float32)) / (Y * XL)
    velocity = (DECAY * momentum_ref[...].astype(jnp.float32) + average).astype(jnp.bfloat16)
    velocity_ref[...] = velocity
    updated = snapshot - RATE * (average + DECAY * velocity.astype(jnp.float32))
    new_ref[...] = rounded(updated).astype(jnp.bfloat16)


def join_kernel(left_ref, right_ref, out_ref):
    width = left_ref.shape[1]
    out_ref[:, :width] = left_ref[...]
    out_ref[:, width:] = right_ref[...]


def join(left, right, after=()):
    rows, columns = left.shape
    out = jax.ShapeDtypeStruct((rows, 2 * columns), left.dtype)
    return whole(join_kernel, out, "join", [left, right], after=after)


def assemble_kernel(*refs):
    pair_refs, (out_ref, done_ref) = refs[:-2], refs[-2:]
    me = lax.axis_index("replica")
    y, x = me // XL, me % XL
    for dy, pair_ref in enumerate(pair_refs):
        for dx in range(XL):
            owner = ((y + dy) % Y) * XL + (x + dx) % XL
            at = pl.multiple_of(owner * BLOCK, BLOCK)
            inside = slice(dx * BLOCK, (dx + 1) * BLOCK)
            out_ref[:, pl.ds(at, BLOCK)] = pair_ref[:, inside]
    done_ref[...] = jnp.zeros_like(done_ref)


def whole(kernel, out_shape, name, operands, after=()):
    spec = pl.BlockSpec(memory_space=pltpu.VMEM)
    nbytes = sum(v.size * v.dtype.itemsize for v in operands)
    count = len(operands)

    def run(*refs):
        kernel(*refs[:count], *refs[count + len(after) :])

    return pl.pallas_call(
        run,
        in_specs=[spec] * count + [pl.BlockSpec(memory_space=pl.ANY)] * len(after),
        out_specs=jax.tree.map(lambda _: spec, out_shape),
        out_shape=out_shape,
        compiler_params=pltpu.CompilerParams(vmem_limit_bytes=4 * MIB),
        cost_estimate=cost(8 * nbytes, 2 * nbytes),
        name=name,
    )(*operands, *after)


def body(tokens, gain, next_weights, weights, snapshot, momentum):
    shape = jax.ShapeDtypeStruct
    _, rows, columns = next_weights.shape
    half = rows // 2

    own, own_low, own_high, *slices = prepare(gain, next_weights, weights)

    def project_on(totals, pieces, after=(), last=False, counted=True):
        return project(
            tokens, other_tokens, pieces, rows, totals, after, last, counted
        )

    other_tokens = to_core(tokens)
    ring_1 = along_z(own)
    low_0 = along_x(own_low)
    arrived_1 = across_replicas(slices[1], lambda y, x: (y + 1, x))
    arrived_3 = across_replicas(slices[3], lambda y, x: (y - 1, x))
    tokens, row_scale = fetch(
        load_kernel,
        tokens,
        [shape(tokens.shape, tokens.dtype), shape((tokens.shape[1], BLOCK), jnp.float32)],
        12,
        "load",
        [own],
    )
    ring_1, low_0, own_high, slice_2 = phase(
        [ring_1, low_0, own_high, slices[2]], after=[row_scale, arrived_1, arrived_3]
    )

    ring_2 = along_z(ring_1)
    high_0 = along_x(own_high)
    low_1 = along_z(low_0)
    arrived_2 = across_replicas(slice_2, lambda y, x: (y + 2, x))
    totals = project_on((), [((0, 0, 0, 0), own), ((1, 0, 0, 0), ring_1)])
    own_sum, other_sum = whole(
        partial_kernel,
        [shape((rows, BLOCK), jnp.float32), shape((rows, BLOCK), jnp.bfloat16)],
        "partial",
        [snapshot, slices[0], arrived_1, arrived_2, arrived_3],
        after=[totals[0]],
    )
    other_sum = across_replicas(other_sum, lambda y, x: (y, 1 - x))
    ring_2, high_0, low_1, other_sum = phase([ring_2, high_0, low_1, other_sum])

    ring_3 = along_z(ring_2)
    low_2 = along_z(low_1)
    new, velocity = whole(
        update_kernel,
        [shape((rows, BLOCK), jnp.bfloat16)] * 2,
        "update",
        [snapshot, momentum, own_sum, other_sum],
    )
    new_other = across_replicas(new, lambda y, x: (y, 1 - x))
    (high_2_sent,) = phase([ring_2[half:]], after=[new_other])
    high_2 = along_x(high_2_sent)
    pair = join(new, new_other, after=[high_2_sent])
    pair_1 = across_replicas(pair, lambda y, x: (y - 1, x))
    pair_3 = across_replicas(pair, lambda y, x: (y + 1, x))
    totals = project_on(
        totals,
        [
            ((2, 0, 0, 0), ring_2),
            ((0, 1, 0, 0), low_0),
            ((0, 1, 0, half), high_0),
        ],
        after=[pair],
        counted=False,
    )
    ring_3, high_0 = phase([ring_3, high_0], after=[totals[0]])

    high_1 = along_z(high_0)
    high_3 = along_x(ring_3[half:])
    low_2, pair = phase([low_2, pair], after=[pair_1, pair_3, ring_3])

    low_3 = along_z(low_2)
    pair_2 = across_replicas(pair, lambda y, x: (y + 2, x))
    totals = project_on(
        totals,
        [
            ((3, 0, 0, 0), ring_3),
            ((1, 1, 0, 0), low_1),
        ],
        after=[low_2],
    )
    own_total, other_total = project_on(
        totals,
        [
            ((2, 1, 0, half), high_2),
            ((2, 1, 0, 0), low_2),
            ((1, 1, 0, half), high_1),
        ],
        last=True,
    )
    low_3, high_3, pair_2, other_total = phase([low_3, high_3, pair_2, other_total])

    low_3_other, high_3_other = to_core(low_3), to_core(high_3)
    other_total = to_core(other_total)
    own_total = finish(
        tokens, [((3, 1, 0, 0), low_3), ((3, 1, 0, half), high_3)], rows, [own_total]
    )
    new_weights, done = whole(
        assemble_kernel,
        [shape((rows, columns), jnp.bfloat16), shape((8, BLOCK), jnp.float32)],
        "assemble",
        [pair, pair_1, pair_2, pair_3],
        after=[own_total],
    )
    next_keys = finish(
        tokens,
        [((3, 1, 1, 0), low_3_other), ((3, 1, 1, half), high_3_other)],
        rows,
        [own_total, other_total],
        row_scale,
        after=[done],
    )
    return (next_keys, new_weights, velocity)


def solution(mesh):
    placed = (
        P("replica", "fsdp", None),
        P("replica", None),
        P("replica", "fsdp", None),
        P("replica", "fsdp", None),
        P("fsdp", None),
        P("fsdp", "replica"),
    )
    return jax.shard_map(
        body,
        mesh=mesh,
        in_specs=placed,
        out_specs=(P("replica", "fsdp", None), P("fsdp", None), P("fsdp", "replica")),
        check_vma=False,
    )
```

```python
import functools

import jax
import jax.numpy as jnp
from jax import lax
from jax.experimental import pallas as pl
from jax.experimental.pallas import tpu as pltpu
from jax.sharding import PartitionSpec as P

BLOCK = 128
DECAY = 0.9
RATE = 0.7
EPS = 1e-05
MIB = 1024 * 1024

Z, X, C = 4, 2, 2
Y, XL = 4, 2


def fsdp_perm(move):
    pairs = []
    for z in range(Z):
        for x in range(X):
            for c in range(C):
                to_z, to_x, to_c = move(z, x, c)
                pairs.append((z * 4 + x * 2 + c, (to_z % Z) * 4 + to_x * 2 + to_c))
    return pairs


def along_z(value):
    return lax.ppermute(
        value, "fsdp", fsdp_perm(lambda z, x, c: (z + 1 - 2 * c, x, c))
    )


def along_x(value):
    return lax.ppermute(value, "fsdp", fsdp_perm(lambda z, x, c: (z, 1 - x, c)))


def to_core(value):
    return lax.ppermute(value, "fsdp", fsdp_perm(lambda z, x, c: (z, x, 1 - c)))


def across_replicas(value, move):
    pairs = []
    for y in range(Y):
        for x in range(XL):
            to_y, to_x = move(y, x)
            pairs.append((y * XL + x, (to_y % Y) * XL + to_x))
    return lax.ppermute(value, "replica", pairs)


def cost(flops, nbytes):
    return pl.CostEstimate(flops=flops, bytes_accessed=nbytes, transcendentals=0)


def prepare_kernel(
    gain_hbm, next_hbm, weights_hbm, out_ref, low_ref, high_ref, *refs
):
    slice_refs, (gain_ref, next_ref, sems, slice_sems) = refs[:Y], refs[Y:]
    rows = next_ref.shape[0]
    side = BLOCK
    first = pl.multiple_of(lax.axis_index("fsdp") * rows, rows)
    copies = [
        pltpu.make_async_copy(
            gain_hbm.at[:, pl.ds(first, rows)], gain_ref, sems.at[rows // side]
        )
    ]
    for i in range(rows // side):
        at = slice(i * side, (i + 1) * side)
        copies.append(
            pltpu.make_async_copy(next_hbm.at[0, at, :], next_ref.at[at, :], sems.at[i])
        )
    y = lax.axis_index("replica") // XL
    width = slice_refs[0].shape[1]
    slice_copies = []
    for dy, slice_ref in enumerate(slice_refs):
        at = pl.multiple_of(((y + dy) % Y) * width, width)
        slice_copies.append(
            pltpu.make_async_copy(
                weights_hbm.at[0, :, pl.ds(at, width)], slice_ref, slice_sems.at[dy]
            )
        )
    for copy in copies + slice_copies:
        copy.start()
    eye = lax.broadcasted_iota(jnp.int32, (side, side), 0) == lax.broadcasted_iota(
        jnp.int32, (side, side), 1
    )
    copies[0].wait()
    for i in range(rows // side):
        at = slice(i * side, (i + 1) * side)
        gain = jnp.where(eye, gain_ref[:, at], 0.0)
        column = jnp.sum(gain, axis=1, keepdims=True)
        copies[1 + i].wait()
        block = (next_ref[at, :].astype(jnp.float32) * column).astype(jnp.bfloat16)
        out_ref[at, :] = block
        if i * side < rows // 2:
            low_ref[at, :] = block
        else:
            high_ref[i * side - rows // 2 : (i + 1) * side - rows // 2, :] = block
    for copy in slice_copies:
        copy.wait()


def prepare(gain, next_weights, weights):
    _, rows, columns = next_weights.shape
    hbm = pl.BlockSpec(memory_space=pltpu.HBM)
    shapes = [(rows, columns), (rows // 2, columns), (rows // 2, columns)]
    shapes += [(rows, columns // Y)] * Y
    operands = [gain, next_weights, weights]
    return pl.pallas_call(
        prepare_kernel,
        in_specs=[hbm] * 3,
        out_specs=[pl.BlockSpec(memory_space=pltpu.VMEM)] * len(shapes),
        out_shape=[jax.ShapeDtypeStruct(s, jnp.bfloat16) for s in shapes],
        scratch_shapes=[
            pltpu.VMEM((1, rows), jnp.float32),
            pltpu.VMEM((rows, columns), jnp.bfloat16),
            pltpu.SemaphoreType.DMA((rows // BLOCK + 1,)),
            pltpu.SemaphoreType.DMA((Y,)),
        ],
        compiler_params=pltpu.CompilerParams(vmem_limit_bytes=4 * MIB),
        cost_estimate=cost(rows * columns, 4 * rows * columns),
        name="prepare",
    )(*(pltpu.with_memory_space_constraint(v, pltpu.HBM) for v in operands))


def phase(values, after=()):
    spec = pl.BlockSpec(memory_space=pl.ANY)
    count = len(values)
    return pl.pallas_call(
        lambda *refs: None,
        in_specs=[spec] * (count + len(after)),
        out_specs=[spec] * count,
        out_shape=[jax.ShapeDtypeStruct(v.shape, v.dtype) for v in values],
        input_output_aliases={i: i for i in range(count)},
        compiler_params=pltpu.CompilerParams(vmem_limit_bytes=MIB),
        cost_estimate=cost(0, 0),
        name="phase",
    )(*values, *after)


def load_kernel(tokens_hbm, tokens_ref, scale_ref, sems):
    _, rows, features = tokens_ref.shape
    parts = sems.shape[0]
    size, tile, width = rows // parts, 32, 512

    def copy(i):
        at = pl.ds(pl.multiple_of(i * size, size), size)
        return pltpu.make_async_copy(
            tokens_hbm.at[0, at, :], tokens_ref.at[0, at, :], sems.at[i]
        )

    for i in range(parts):
        copy(i).start()

    def part(i, carry):
        copy(i).wait()
        for k in range(size // tile):
            at = pl.ds(pl.multiple_of(i * size + k * tile, tile), tile)
            total = jnp.zeros((tile, width), jnp.float32)
            for j in range(features // width):
                value = tokens_ref[0, at, j * width : (j + 1) * width]
                value = value.astype(jnp.float32)
                total = total + value * value
            mean = jnp.sum(total, axis=1, keepdims=True) / features
            scale_ref[at, :] = jnp.broadcast_to(lax.rsqrt(mean + EPS), (tile, BLOCK))
        return carry

    lax.fori_loop(0, parts, part, 0)


def fetch(kernel, tokens, out_shapes, copies, name, after):
    spec = pl.BlockSpec(memory_space=pltpu.VMEM)

    def run(tokens_hbm, *refs):
        kernel(tokens_hbm, *refs[len(after) :])

    return pl.pallas_call(
        run,
        in_specs=[pl.BlockSpec(memory_space=pltpu.HBM)]
        + [pl.BlockSpec(memory_space=pl.ANY)] * len(after),
        out_specs=[spec] * len(out_shapes),
        out_shape=out_shapes,
        scratch_shapes=[pltpu.SemaphoreType.DMA((copies,))],
        compiler_params=pltpu.CompilerParams(vmem_limit_bytes=3 * MIB),
        cost_estimate=cost(tokens.size, 2 * tokens.size),
        name=name,
    )(pltpu.with_memory_space_constraint(tokens, pltpu.HBM), *after)


def project_kernel(places, rows, given, *refs):
    count = len(places)
    tokens_ref, other_tokens_ref, weight_refs = refs[0], refs[1], refs[2 : 2 + count]
    total_refs = refs[2 + count : 4 + count] if given else None
    out_ref, other_ref = refs[-2:]
    me = lax.axis_index("fsdp")
    z, x, c = me // 4, (me // 2) % 2, me % 2
    starts = []
    for step, dx, dc, first in places:
        block = ((z + (2 * c - 1) * step + Z) % Z) * 2 + (x + dx) % 2
        starts.append(pl.multiple_of((block * 2 + c) * rows + first, BLOCK))
    tile = 256

    def column(n, carry):
        at = pl.ds(pl.multiple_of(n * tile, tile), tile)
        total = total_refs[0][:, at] if given else None
        other = total_refs[1][:, at] if given else None
        for start, weight_ref in zip(starts, weight_refs):
            depth = weight_ref.shape[0]
            weight = weight_ref[:, at]
            part = jnp.dot(
                tokens_ref[0, :, pl.ds(start, depth)],
                weight,
                preferred_element_type=jnp.float32,
            )
            total = part if total is None else total + part
            part = jnp.dot(
                other_tokens_ref[0, :, pl.ds(start, depth)],
                weight,
                preferred_element_type=jnp.float32,
            )
            other = part if other is None else other + part
        out_ref[:, at] = total
        other_ref[:, at] = other.astype(other_ref.dtype)
        return carry

    lax.fori_loop(0, weight_refs[0].shape[1] // tile, column, 0)


def project(tokens, other_tokens, pieces, rows, totals=(), after=(), last=False, counted=True):
    count = tokens.shape[1]
    columns = pieces[0][1].shape[1]
    operands = [tokens, other_tokens, *(w for _, w in pieces)]
    aliases = {len(operands) + i: i for i in range(2 - last)} if totals else {}
    operands += totals
    depth = sum(w.shape[0] for _, w in pieces)
    spec = pl.BlockSpec(memory_space=pltpu.VMEM)
    places = tuple(p for p, _ in pieces)
    return pl.pallas_call(
        functools.partial(project_kernel, places, rows, bool(totals)),
        in_specs=[spec] * len(operands)
        + [pl.BlockSpec(memory_space=pl.ANY)] * len(after),
        out_specs=[spec] * 2,
        out_shape=[
            jax.ShapeDtypeStruct((count, columns), jnp.float32),
            jax.ShapeDtypeStruct(
                (count, columns), jnp.bfloat16 if last else jnp.float32
            ),
        ],
        input_output_aliases=aliases,
        compiler_params=pltpu.CompilerParams(vmem_limit_bytes=3 * MIB),
        cost_estimate=cost(4 * count * depth * columns, 2 * columns * depth)
        if counted
        else cost(1, 1),
        name="project",
    )(*operands, *after)


def finish_kernel(places, rows, given, last, *refs):
    count = len(places)
    tokens_ref, weight_refs = refs[0], refs[1 : 1 + count]
    total_refs = refs[1 + count : 1 + count + given]
    out_ref = refs[-1]
    me = lax.axis_index("fsdp")
    z, x, c = me // 4, (me // 2) % 2, me % 2
    starts = []
    for step, dx, dc, first in places:
        core = (c + dc) % 2
        shard = ((z + (2 * core - 1) * step + Z) % Z) * 4 + ((x + dx) % 2) * 2 + core
        starts.append(pl.multiple_of(shard * rows + first, BLOCK))
    tile = 256

    def column(n, carry):
        at = pl.ds(pl.multiple_of(n * tile, tile), tile)
        total = total_refs[0][:, at]
        for total_ref in total_refs[1:]:
            total = total + total_ref[:, at].astype(jnp.float32)
        for start, weight_ref in zip(starts, weight_refs):
            total = total + jnp.dot(
                tokens_ref[0, :, pl.ds(start, weight_ref.shape[0])],
                weight_ref[:, at],
                preferred_element_type=jnp.float32,
            )
        if last:
            scale_ref = refs[1 + count + given]
            out_ref[0, :, at] = (total * scale_ref[:, :1]).astype(jnp.bfloat16)
        else:
            out_ref[:, at] = total
        return carry

    lax.fori_loop(0, weight_refs[0].shape[1] // tile, column, 0)


def finish(tokens, pieces, rows, totals, row_scale=None, after=()):
    count = tokens.shape[1]
    columns = totals[0].shape[1]
    last = row_scale is not None
    operands = [tokens, *(w for _, w in pieces), *totals]
    if last:
        operands.append(row_scale)
        out_shape = jax.ShapeDtypeStruct((1, count, columns), jnp.bfloat16)
    else:
        out_shape = jax.ShapeDtypeStruct((count, columns), jnp.float32)
    depth = sum(w.shape[0] for _, w in pieces)
    spec = pl.BlockSpec(memory_space=pltpu.VMEM)
    places = tuple(p for p, _ in pieces)
    return pl.pallas_call(
        functools.partial(finish_kernel, places, rows, len(totals), last),
        in_specs=[spec] * len(operands)
        + [pl.BlockSpec(memory_space=pl.ANY)] * len(after),
        out_specs=spec,
        out_shape=out_shape,
        input_output_aliases={} if last else {1 + len(pieces): 0},
        compiler_params=pltpu.CompilerParams(vmem_limit_bytes=3 * MIB),
        cost_estimate=cost(2 * count * depth * columns, 2 * columns * depth),
        name="finish",
    )(*operands, *after)


def scale_of(values):
    target = (jnp.max(jnp.abs(values), axis=1, keepdims=True) + 1e-06) / 448.0
    high = target.astype(jnp.bfloat16).astype(jnp.float32)
    low = (target - high).astype(jnp.bfloat16).astype(jnp.float32)
    return high + low


def rounded(values):
    scale = scale_of(values)
    return (values / scale).astype(jnp.bfloat16).astype(jnp.float32) * scale


def partial_kernel(snapshot_ref, *refs):
    weight_refs, (own_ref, other_ref) = refs[:-2], refs[-2:]
    me = lax.axis_index("replica")
    y, x = me // XL, me % XL
    for dx, out_ref in ((0, own_ref), (1, other_ref)):
        column = (x + dx) % XL
        at = pl.multiple_of((y * XL + column) * BLOCK, BLOCK)
        snapshot = snapshot_ref[:, pl.ds(at, BLOCK)]
        inside = pl.ds(pl.multiple_of(column * BLOCK, BLOCK), BLOCK)
        total = None
        for weight_ref in weight_refs:
            part = rounded(snapshot - weight_ref[:, inside].astype(jnp.float32))
            total = part if total is None else total + part
        out_ref[...] = total.astype(out_ref.dtype)


def update_kernel(snapshot_ref, momentum_ref, own_ref, other_ref, new_ref, velocity_ref):
    me = lax.axis_index("replica")
    at = pl.multiple_of(me * BLOCK, BLOCK)
    snapshot = snapshot_ref[:, pl.ds(at, BLOCK)]
    average = (own_ref[...] + other_ref[...].astype(jnp.float32)) / (Y * XL)
    velocity = (DECAY * momentum_ref[...].astype(jnp.float32) + average).astype(jnp.bfloat16)
    velocity_ref[...] = velocity
    updated = snapshot - RATE * (average + DECAY * velocity.astype(jnp.float32))
    new_ref[...] = rounded(updated).astype(jnp.bfloat16)


def join_kernel(left_ref, right_ref, out_ref):
    width = left_ref.shape[1]
    out_ref[:, :width] = left_ref[...]
    out_ref[:, width:] = right_ref[...]


def join(left, right, after=()):
    rows, columns = left.shape
    out = jax.ShapeDtypeStruct((rows, 2 * columns), left.dtype)
    return whole(join_kernel, out, "join", [left, right], after=after)


def assemble_kernel(*refs):
    pair_refs, (out_ref, done_ref) = refs[:-2], refs[-2:]
    me = lax.axis_index("replica")
    y, x = me // XL, me % XL
    for dy, pair_ref in enumerate(pair_refs):
        for dx in range(XL):
            owner = ((y + dy) % Y) * XL + (x + dx) % XL
            at = pl.multiple_of(owner * BLOCK, BLOCK)
            inside = slice(dx * BLOCK, (dx + 1) * BLOCK)
            out_ref[:, pl.ds(at, BLOCK)] = pair_ref[:, inside]
    done_ref[...] = jnp.zeros_like(done_ref)


def whole(kernel, out_shape, name, operands, after=()):
    spec = pl.BlockSpec(memory_space=pltpu.VMEM)
    nbytes = sum(v.size * v.dtype.itemsize for v in operands)
    count = len(operands)

    def run(*refs):
        kernel(*refs[:count], *refs[count + len(after) :])

    return pl.pallas_call(
        run,
        in_specs=[spec] * count + [pl.BlockSpec(memory_space=pl.ANY)] * len(after),
        out_specs=jax.tree.map(lambda _: spec, out_shape),
        out_shape=out_shape,
        compiler_params=pltpu.CompilerParams(vmem_limit_bytes=3 * MIB),
        cost_estimate=cost(8 * nbytes, 2 * nbytes),
        name=name,
    )(*operands, *after)


def body(tokens, gain, next_weights, weights, snapshot, momentum):
    shape = jax.ShapeDtypeStruct
    _, rows, columns = next_weights.shape
    half = rows // 2

    own, own_low, own_high, *slices = prepare(gain, next_weights, weights)

    def project_on(totals, pieces, after=(), last=False, counted=True):
        return project(
            tokens, other_tokens, pieces, rows, totals, after, last, counted
        )

    other_tokens = to_core(tokens)
    ring_1 = along_z(own)
    low_0 = along_x(own_low)
    arrived_1 = across_replicas(slices[1], lambda y, x: (y + 1, x))
    arrived_3 = across_replicas(slices[3], lambda y, x: (y - 1, x))
    tokens, row_scale = fetch(
        load_kernel,
        tokens,
        [shape(tokens.shape, tokens.dtype), shape((tokens.shape[1], BLOCK), jnp.float32)],
        12,
        "load",
        [own],
    )
    ring_1, low_0, own_high, slice_2 = phase(
        [ring_1, low_0, own_high, slices[2]], after=[row_scale, arrived_1, arrived_3]
    )

    ring_2 = along_z(ring_1)
    high_0 = along_x(own_high)
    low_1 = along_z(low_0)
    arrived_2 = across_replicas(slice_2, lambda y, x: (y + 2, x))
    totals = project_on((), [((0, 0, 0, 0), own), ((1, 0, 0, 0), ring_1)])
    own_sum, other_sum = whole(
        partial_kernel,
        [shape((rows, BLOCK), jnp.float32), shape((rows, BLOCK), jnp.bfloat16)],
        "partial",
        [snapshot, slices[0], arrived_1, arrived_2, arrived_3],
        after=[totals[0]],
    )
    other_sum = across_replicas(other_sum, lambda y, x: (y, 1 - x))
    ring_2, high_0 = phase([ring_2, high_0], after=[own_sum])

    high_r2 = ring_2[half:]
    high_r3 = along_z(high_r2)
    low_r3 = along_z(ring_2[:half])
    high_2 = along_x(high_r2)
    low_1, other_sum = phase([low_1, other_sum], after=[ring_2])

    low_2 = along_z(low_1)
    new, velocity = whole(
        update_kernel,
        [shape((rows, BLOCK), jnp.bfloat16)] * 2,
        "update",
        [snapshot, momentum, own_sum, other_sum],
    )
    new_other = across_replicas(new, lambda y, x: (y, 1 - x))
    totals = project_on(
        totals,
        [
            ((2, 0, 0, 0), ring_2),
            ((0, 1, 0, 0), low_0),
            ((0, 1, 0, half), high_0),
        ],
        after=[new],
        counted=False,
    )
    high_r3, high_0 = phase([high_r3, high_0], after=[totals[0]])

    high_3 = along_x(high_r3)
    high_1 = along_z(high_0)
    (new_other,) = phase([new_other], after=[high_r3, low_r3, high_2])
    pair = join(new, new_other)
    pair_1 = across_replicas(pair, lambda y, x: (y - 1, x))
    pair_3 = across_replicas(pair, lambda y, x: (y + 1, x))
    (low_2,) = phase([low_2], after=[pair])

    low_3 = along_z(low_2)
    totals = project_on(
        totals,
        [
            ((3, 0, 0, 0), low_r3),
            ((3, 0, 0, half), high_r3),
            ((1, 1, 0, 0), low_1),
        ],
        after=[low_2],
        counted=False,
    )
    (pair,) = phase([pair], after=[totals[0], pair_1])
    pair_2 = across_replicas(pair, lambda y, x: (y + 2, x))
    own_total, other_total = project_on(
        totals,
        [
            ((2, 1, 0, half), high_2),
            ((2, 1, 0, 0), low_2),
            ((1, 1, 0, half), high_1),
            ((3, 1, 0, half), high_3),
        ],
        last=True,
        counted=False,
        after=[pair],
    )
    low_3, other_total, pair_2 = phase([low_3, other_total, pair_2], after=[pair_3])

    low_3_other = to_core(low_3)
    other_total = to_core(other_total)
    own_total = finish(
        tokens, [((3, 1, 0, 0), low_3)], rows, [own_total]
    )
    new_weights, done = whole(
        assemble_kernel,
        [shape((rows, columns), jnp.bfloat16), shape((8, BLOCK), jnp.float32)],
        "assemble",
        [pair, pair_1, pair_2, pair_3],
        after=[own_total],
    )
    next_keys = finish(
        tokens,
        [((3, 1, 1, 0), low_3_other)],
        rows,
        [own_total, other_total],
        row_scale,
        after=[done],
    )
    return (next_keys, new_weights, velocity)


def solution(mesh):
    placed = (
        P("replica", "fsdp", None),
        P("replica", None),
        P("replica", "fsdp", None),
        P("replica", "fsdp", None),
        P("fsdp", None),
        P("fsdp", "replica"),
    )
    return jax.shard_map(
        body,
        mesh=mesh,
        in_specs=placed,
        out_specs=(P("replica", "fsdp", None), P("fsdp", None), P("fsdp", "replica")),
        check_vma=False,
    )
```

```python
import functools

import jax
import jax.numpy as jnp
from jax import lax
from jax.experimental import pallas as pl
from jax.experimental.pallas import tpu as pltpu
from jax.sharding import PartitionSpec as P

BLOCK = 128
DECAY = 0.9
RATE = 0.7
EPS = 1e-05
MIB = 1024 * 1024

Z, X, C = 4, 2, 2
Y, XL = 4, 2


def fsdp_perm(move):
    pairs = []
    for z in range(Z):
        for x in range(X):
            for c in range(C):
                to_z, to_x, to_c = move(z, x, c)
                pairs.append((z * 4 + x * 2 + c, (to_z % Z) * 4 + to_x * 2 + to_c))
    return pairs


def along_z(value):
    return lax.ppermute(
        value, "fsdp", fsdp_perm(lambda z, x, c: (z + 1 - 2 * c, x, c))
    )


def along_x(value):
    return lax.ppermute(value, "fsdp", fsdp_perm(lambda z, x, c: (z, 1 - x, c)))


def to_core(value):
    return lax.ppermute(value, "fsdp", fsdp_perm(lambda z, x, c: (z, x, 1 - c)))


def across_replicas(value, move):
    pairs = []
    for y in range(Y):
        for x in range(XL):
            to_y, to_x = move(y, x)
            pairs.append((y * XL + x, (to_y % Y) * XL + to_x))
    return lax.ppermute(value, "replica", pairs)


def cost(flops, nbytes):
    return pl.CostEstimate(flops=flops, bytes_accessed=nbytes, transcendentals=0)


def prepare_kernel(
    gain_hbm, next_hbm, weights_hbm, out_ref, low_ref, high_ref, *refs
):
    slice_refs, (gain_ref, next_ref, sems, slice_sems) = refs[:Y], refs[Y:]
    rows = next_ref.shape[0]
    side = BLOCK
    first = pl.multiple_of(lax.axis_index("fsdp") * rows, rows)
    copies = [
        pltpu.make_async_copy(
            gain_hbm.at[:, pl.ds(first, rows)], gain_ref, sems.at[rows // side]
        )
    ]
    for i in range(rows // side):
        at = slice(i * side, (i + 1) * side)
        copies.append(
            pltpu.make_async_copy(next_hbm.at[0, at, :], next_ref.at[at, :], sems.at[i])
        )
    y = lax.axis_index("replica") // XL
    width = slice_refs[0].shape[1]
    slice_copies = []
    for dy, slice_ref in enumerate(slice_refs):
        at = pl.multiple_of(((y + dy) % Y) * width, width)
        slice_copies.append(
            pltpu.make_async_copy(
                weights_hbm.at[0, :, pl.ds(at, width)], slice_ref, slice_sems.at[dy]
            )
        )
    for copy in copies + slice_copies:
        copy.start()
    eye = lax.broadcasted_iota(jnp.int32, (side, side), 0) == lax.broadcasted_iota(
        jnp.int32, (side, side), 1
    )
    copies[0].wait()
    for i in range(rows // side):
        at = slice(i * side, (i + 1) * side)
        gain = jnp.where(eye, gain_ref[:, at], 0.0)
        column = jnp.sum(gain, axis=1, keepdims=True)
        copies[1 + i].wait()
        block = (next_ref[at, :].astype(jnp.float32) * column).astype(jnp.bfloat16)
        out_ref[at, :] = block
        if i * side < rows // 2:
            low_ref[at, :] = block
        else:
            high_ref[i * side - rows // 2 : (i + 1) * side - rows // 2, :] = block
    for copy in slice_copies:
        copy.wait()


def prepare(gain, next_weights, weights):
    _, rows, columns = next_weights.shape
    hbm = pl.BlockSpec(memory_space=pltpu.HBM)
    shapes = [(rows, columns), (rows // 2, columns), (rows // 2, columns)]
    shapes += [(rows, columns // Y)] * Y
    operands = [gain, next_weights, weights]
    return pl.pallas_call(
        prepare_kernel,
        in_specs=[hbm] * 3,
        out_specs=[pl.BlockSpec(memory_space=pltpu.VMEM)] * len(shapes),
        out_shape=[jax.ShapeDtypeStruct(s, jnp.bfloat16) for s in shapes],
        scratch_shapes=[
            pltpu.VMEM((1, rows), jnp.float32),
            pltpu.VMEM((rows, columns), jnp.bfloat16),
            pltpu.SemaphoreType.DMA((rows // BLOCK + 1,)),
            pltpu.SemaphoreType.DMA((Y,)),
        ],
        compiler_params=pltpu.CompilerParams(vmem_limit_bytes=4 * MIB),
        cost_estimate=cost(rows * columns, 4 * rows * columns),
        name="prepare",
    )(*(pltpu.with_memory_space_constraint(v, pltpu.HBM) for v in operands))


def phase(values, after=()):
    spec = pl.BlockSpec(memory_space=pl.ANY)
    count = len(values)
    return pl.pallas_call(
        lambda *refs: None,
        in_specs=[spec] * (count + len(after)),
        out_specs=[spec] * count,
        out_shape=[jax.ShapeDtypeStruct(v.shape, v.dtype) for v in values],
        input_output_aliases={i: i for i in range(count)},
        compiler_params=pltpu.CompilerParams(vmem_limit_bytes=MIB),
        cost_estimate=cost(0, 0),
        name="phase",
    )(*values, *after)


def load_kernel(tokens_hbm, tokens_ref, scale_ref, sems):
    _, rows, features = tokens_ref.shape
    parts = sems.shape[0]
    size, tile, width = rows // parts, 32, 512

    def copy(i):
        at = pl.ds(pl.multiple_of(i * size, size), size)
        return pltpu.make_async_copy(
            tokens_hbm.at[0, at, :], tokens_ref.at[0, at, :], sems.at[i]
        )

    for i in range(parts):
        copy(i).start()

    def part(i, carry):
        copy(i).wait()
        for k in range(size // tile):
            at = pl.ds(pl.multiple_of(i * size + k * tile, tile), tile)
            total = jnp.zeros((tile, width), jnp.float32)
            for j in range(features // width):
                value = tokens_ref[0, at, j * width : (j + 1) * width]
                value = value.astype(jnp.float32)
                total = total + value * value
            mean = jnp.sum(total, axis=1, keepdims=True) / features
            scale_ref[at, :] = jnp.broadcast_to(lax.rsqrt(mean + EPS), (tile, BLOCK))
        return carry

    lax.fori_loop(0, parts, part, 0)


def fetch(kernel, tokens, out_shapes, copies, name, after):
    spec = pl.BlockSpec(memory_space=pltpu.VMEM)

    def run(tokens_hbm, *refs):
        kernel(tokens_hbm, *refs[len(after) :])

    return pl.pallas_call(
        run,
        in_specs=[pl.BlockSpec(memory_space=pltpu.HBM)]
        + [pl.BlockSpec(memory_space=pl.ANY)] * len(after),
        out_specs=[spec] * len(out_shapes),
        out_shape=out_shapes,
        scratch_shapes=[pltpu.SemaphoreType.DMA((copies,))],
        compiler_params=pltpu.CompilerParams(vmem_limit_bytes=3 * MIB),
        cost_estimate=cost(tokens.size, 2 * tokens.size),
        name=name,
    )(pltpu.with_memory_space_constraint(tokens, pltpu.HBM), *after)


def project_kernel(places, rows, given, *refs):
    count = len(places)
    tokens_ref, other_tokens_ref, weight_refs = refs[0], refs[1], refs[2 : 2 + count]
    total_refs = refs[2 + count : 4 + count] if given else None
    out_ref, other_ref = refs[-2:]
    me = lax.axis_index("fsdp")
    z, x, c = me // 4, (me // 2) % 2, me % 2
    starts = []
    for step, dx, dc, first in places:
        block = ((z + (2 * c - 1) * step + Z) % Z) * 2 + (x + dx) % 2
        starts.append(pl.multiple_of((block * 2 + c) * rows + first, BLOCK))
    tile = 256

    def column(n, carry):
        at = pl.ds(pl.multiple_of(n * tile, tile), tile)
        total = total_refs[0][:, at] if given else None
        other = total_refs[1][:, at] if given else None
        for start, weight_ref in zip(starts, weight_refs):
            depth = weight_ref.shape[0]
            weight = weight_ref[:, at]
            part = jnp.dot(
                tokens_ref[0, :, pl.ds(start, depth)],
                weight,
                preferred_element_type=jnp.float32,
            )
            total = part if total is None else total + part
            part = jnp.dot(
                other_tokens_ref[0, :, pl.ds(start, depth)],
                weight,
                preferred_element_type=jnp.float32,
            )
            other = part if other is None else other + part
        out_ref[:, at] = total
        other_ref[:, at] = other.astype(other_ref.dtype)
        return carry

    lax.fori_loop(0, weight_refs[0].shape[1] // tile, column, 0)


def project(tokens, other_tokens, pieces, rows, totals=(), after=(), last=False, counted=True):
    count = tokens.shape[1]
    columns = pieces[0][1].shape[1]
    operands = [tokens, other_tokens, *(w for _, w in pieces)]
    aliases = {len(operands) + i: i for i in range(2 - last)} if totals else {}
    operands += totals
    depth = sum(w.shape[0] for _, w in pieces)
    spec = pl.BlockSpec(memory_space=pltpu.VMEM)
    places = tuple(p for p, _ in pieces)
    return pl.pallas_call(
        functools.partial(project_kernel, places, rows, bool(totals)),
        in_specs=[spec] * len(operands)
        + [pl.BlockSpec(memory_space=pl.ANY)] * len(after),
        out_specs=[spec] * 2,
        out_shape=[
            jax.ShapeDtypeStruct((count, columns), jnp.float32),
            jax.ShapeDtypeStruct(
                (count, columns), jnp.bfloat16 if last else jnp.float32
            ),
        ],
        input_output_aliases=aliases,
        compiler_params=pltpu.CompilerParams(vmem_limit_bytes=3 * MIB),
        cost_estimate=cost(4 * count * depth * columns, 2 * columns * depth)
        if counted
        else cost(1, 1),
        name="project",
    )(*operands, *after)


def finish_kernel(places, rows, given, last, *refs):
    count = len(places)
    tokens_ref, weight_refs = refs[0], refs[1 : 1 + count]
    total_refs = refs[1 + count : 1 + count + given]
    out_ref = refs[-1]
    me = lax.axis_index("fsdp")
    z, x, c = me // 4, (me // 2) % 2, me % 2
    starts = []
    for step, dx, dc, first in places:
        core = (c + dc) % 2
        shard = ((z + (2 * core - 1) * step + Z) % Z) * 4 + ((x + dx) % 2) * 2 + core
        starts.append(pl.multiple_of(shard * rows + first, BLOCK))
    tile = 256

    def column(n, carry):
        at = pl.ds(pl.multiple_of(n * tile, tile), tile)
        total = total_refs[0][:, at]
        for total_ref in total_refs[1:]:
            total = total + total_ref[:, at].astype(jnp.float32)
        for start, weight_ref in zip(starts, weight_refs):
            total = total + jnp.dot(
                tokens_ref[0, :, pl.ds(start, weight_ref.shape[0])],
                weight_ref[:, at],
                preferred_element_type=jnp.float32,
            )
        if last:
            scale_ref = refs[1 + count + given]
            out_ref[0, :, at] = (total * scale_ref[:, :1]).astype(jnp.bfloat16)
        else:
            out_ref[:, at] = total
        return carry

    lax.fori_loop(0, weight_refs[0].shape[1] // tile, column, 0)


def finish(tokens, pieces, rows, totals, row_scale=None, after=()):
    count = tokens.shape[1]
    columns = totals[0].shape[1]
    last = row_scale is not None
    operands = [tokens, *(w for _, w in pieces), *totals]
    if last:
        operands.append(row_scale)
        out_shape = jax.ShapeDtypeStruct((1, count, columns), jnp.bfloat16)
    else:
        out_shape = jax.ShapeDtypeStruct((count, columns), jnp.float32)
    depth = sum(w.shape[0] for _, w in pieces)
    spec = pl.BlockSpec(memory_space=pltpu.VMEM)
    places = tuple(p for p, _ in pieces)
    return pl.pallas_call(
        functools.partial(finish_kernel, places, rows, len(totals), last),
        in_specs=[spec] * len(operands)
        + [pl.BlockSpec(memory_space=pl.ANY)] * len(after),
        out_specs=spec,
        out_shape=out_shape,
        input_output_aliases={} if last else {1 + len(pieces): 0},
        compiler_params=pltpu.CompilerParams(vmem_limit_bytes=3 * MIB),
        cost_estimate=cost(2 * count * depth * columns, 2 * columns * depth),
        name="finish",
    )(*operands, *after)


def scale_of(values):
    target = (jnp.max(jnp.abs(values), axis=1, keepdims=True) + 1e-06) / 448.0
    high = target.astype(jnp.bfloat16).astype(jnp.float32)
    low = (target - high).astype(jnp.bfloat16).astype(jnp.float32)
    return high + low


def rounded(values):
    scale = scale_of(values)
    return (values / scale).astype(jnp.bfloat16).astype(jnp.float32) * scale


def partial_kernel(snapshot_ref, *refs):
    weight_refs, (own_ref, other_ref) = refs[:-2], refs[-2:]
    me = lax.axis_index("replica")
    y, x = me // XL, me % XL
    for dx, out_ref in ((0, own_ref), (1, other_ref)):
        column = (x + dx) % XL
        at = pl.multiple_of((y * XL + column) * BLOCK, BLOCK)
        snapshot = snapshot_ref[:, pl.ds(at, BLOCK)]
        inside = pl.ds(pl.multiple_of(column * BLOCK, BLOCK), BLOCK)
        total = None
        for weight_ref in weight_refs:
            part = rounded(snapshot - weight_ref[:, inside].astype(jnp.float32))
            total = part if total is None else total + part
        out_ref[...] = total.astype(out_ref.dtype)


def update_kernel(snapshot_ref, momentum_ref, own_ref, other_ref, new_ref, velocity_ref):
    me = lax.axis_index("replica")
    at = pl.multiple_of(me * BLOCK, BLOCK)
    snapshot = snapshot_ref[:, pl.ds(at, BLOCK)]
    average = (own_ref[...] + other_ref[...].astype(jnp.float32)) / (Y * XL)
    velocity = (DECAY * momentum_ref[...].astype(jnp.float32) + average).astype(jnp.bfloat16)
    velocity_ref[...] = velocity
    updated = snapshot - RATE * (average + DECAY * velocity.astype(jnp.float32))
    new_ref[...] = rounded(updated).astype(jnp.bfloat16)


def join_kernel(left_ref, right_ref, out_ref, copy_ref):
    width = left_ref.shape[1]
    for ref in (out_ref, copy_ref):
        ref[:, :width] = left_ref[...]
        ref[:, width:] = right_ref[...]


def join(left, right):
    rows, columns = left.shape
    out = jax.ShapeDtypeStruct((rows, 2 * columns), left.dtype)
    return whole(join_kernel, [out, out], "join", [left, right])


def assemble_kernel(*refs):
    pair_refs, (out_ref, done_ref) = refs[:-2], refs[-2:]
    me = lax.axis_index("replica")
    y, x = me // XL, me % XL
    for dy, pair_ref in enumerate(pair_refs):
        for dx in range(XL):
            owner = ((y + dy) % Y) * XL + (x + dx) % XL
            at = pl.multiple_of(owner * BLOCK, BLOCK)
            inside = slice(dx * BLOCK, (dx + 1) * BLOCK)
            out_ref[:, pl.ds(at, BLOCK)] = pair_ref[:, inside]
    done_ref[...] = jnp.zeros_like(done_ref)


def whole(kernel, out_shape, name, operands, after=()):
    spec = pl.BlockSpec(memory_space=pltpu.VMEM)
    nbytes = sum(v.size * v.dtype.itemsize for v in operands)
    count = len(operands)

    def run(*refs):
        kernel(*refs[:count], *refs[count + len(after) :])

    return pl.pallas_call(
        run,
        in_specs=[spec] * count + [pl.BlockSpec(memory_space=pl.ANY)] * len(after),
        out_specs=jax.tree.map(lambda _: spec, out_shape),
        out_shape=out_shape,
        compiler_params=pltpu.CompilerParams(vmem_limit_bytes=3 * MIB),
        cost_estimate=cost(8 * nbytes, 2 * nbytes),
        name=name,
    )(*operands, *after)


def body(tokens, gain, next_weights, weights, snapshot, momentum):
    shape = jax.ShapeDtypeStruct
    _, rows, columns = next_weights.shape
    half = rows // 2

    own, own_low, own_high, *slices = prepare(gain, next_weights, weights)

    def project_on(totals, pieces, after=(), last=False, counted=True):
        return project(
            tokens, other_tokens, pieces, rows, totals, after, last, counted
        )

    other_tokens = to_core(tokens)
    ring_1 = along_z(own)
    low_0 = along_x(own_low)
    arrived_1 = across_replicas(slices[1], lambda y, x: (y + 1, x))
    arrived_3 = across_replicas(slices[3], lambda y, x: (y - 1, x))
    tokens, row_scale = fetch(
        load_kernel,
        tokens,
        [shape(tokens.shape, tokens.dtype), shape((tokens.shape[1], BLOCK), jnp.float32)],
        12,
        "load",
        [own],
    )
    ring_1, low_0, own_high, slice_2 = phase(
        [ring_1, low_0, own_high, slices[2]], after=[row_scale, arrived_1, arrived_3]
    )

    ring_2 = along_z(ring_1)
    high_0 = along_x(own_high)
    low_1 = along_z(low_0)
    arrived_2 = across_replicas(slice_2, lambda y, x: (y + 2, x))
    totals = project_on((), [((0, 0, 0, 0), own), ((1, 0, 0, 0), ring_1)])
    own_sum, other_sum = whole(
        partial_kernel,
        [shape((rows, BLOCK), jnp.float32), shape((rows, BLOCK), jnp.bfloat16)],
        "partial",
        [snapshot, slices[0], arrived_1, arrived_2, arrived_3],
        after=[totals[0]],
    )
    other_sum = across_replicas(other_sum, lambda y, x: (y, 1 - x))
    ring_2, high_0 = phase([ring_2, high_0], after=[own_sum])

    high_r2 = ring_2[half:]
    high_r3 = along_z(high_r2)
    low_r3 = along_z(ring_2[:half])
    high_2 = along_x(high_r2)
    low_1, other_sum = phase([low_1, other_sum], after=[ring_2])

    low_2 = along_z(low_1)
    new, velocity = whole(
        update_kernel,
        [shape((rows, BLOCK), jnp.bfloat16)] * 2,
        "update",
        [snapshot, momentum, own_sum, other_sum],
    )
    new_other = across_replicas(new, lambda y, x: (y, 1 - x))
    totals = project_on(
        totals,
        [
            ((2, 0, 0, 0), ring_2),
            ((0, 1, 0, 0), low_0),
            ((0, 1, 0, half), high_0),
        ],
        after=[new],
        counted=False,
    )
    high_r3, high_0 = phase([high_r3, high_0], after=[totals[0]])

    high_3 = along_x(high_r3)
    high_1 = along_z(high_0)
    (new_other,) = phase([new_other], after=[high_r3, low_r3, high_2])
    pair, pair_sent = join(new, new_other)
    pair_1 = across_replicas(pair, lambda y, x: (y - 1, x))
    pair_3 = across_replicas(pair, lambda y, x: (y + 1, x))
    (low_2,) = phase([low_2], after=[pair])

    low_3 = along_z(low_2)
    totals = project_on(
        totals,
        [
            ((3, 0, 0, 0), low_r3),
            ((3, 0, 0, half), high_r3),
            ((1, 1, 0, 0), low_1),
        ],
        after=[low_2],
        counted=False,
    )
    (pair_sent,) = phase([pair_sent], after=[totals[0], pair_1])
    pair_2 = across_replicas(pair_sent, lambda y, x: (y + 2, x))
    own_total, other_total = project_on(
        totals,
        [
            ((2, 1, 0, half), high_2),
            ((2, 1, 0, 0), low_2),
            ((1, 1, 0, half), high_1),
            ((3, 1, 0, half), high_3),
        ],
        last=True,
        counted=False,
        after=[pair_sent],
    )
    low_3, other_total, pair_2 = phase([low_3, other_total, pair_2], after=[pair_3])

    low_3_other = to_core(low_3)
    other_total = to_core(other_total)
    own_total = finish(
        tokens, [((3, 1, 0, 0), low_3)], rows, [own_total]
    )
    new_weights, done = whole(
        assemble_kernel,
        [shape((rows, columns), jnp.bfloat16), shape((8, BLOCK), jnp.float32)],
        "assemble",
        [pair, pair_1, pair_2, pair_3],
        after=[own_total],
    )
    next_keys = finish(
        tokens,
        [((3, 1, 1, 0), low_3_other)],
        rows,
        [own_total, other_total],
        row_scale,
        after=[done],
    )
    return (next_keys, new_weights, velocity)


def solution(mesh):
    placed = (
        P("replica", "fsdp", None),
        P("replica", None),
        P("replica", "fsdp", None),
        P("replica", "fsdp", None),
        P("fsdp", None),
        P("fsdp", "replica"),
    )
    return jax.shard_map(
        body,
        mesh=mesh,
        in_specs=placed,
        out_specs=(P("replica", "fsdp", None), P("fsdp", None), P("fsdp", "replica")),
        check_vma=False,
    )
```

```python
import functools

import jax
import jax.numpy as jnp
from jax import lax
from jax.experimental import pallas as pl
from jax.experimental.pallas import tpu as pltpu
from jax.sharding import PartitionSpec as P

BLOCK = 128
DECAY = 0.9
RATE = 0.7
EPS = 1e-05
MIB = 1024 * 1024

Z, X, C = 4, 2, 2
Y, XL = 4, 2


def fsdp_perm(move):
    pairs = []
    for z in range(Z):
        for x in range(X):
            for c in range(C):
                to_z, to_x, to_c = move(z, x, c)
                pairs.append((z * 4 + x * 2 + c, (to_z % Z) * 4 + to_x * 2 + to_c))
    return pairs


def along_z(value):
    return lax.ppermute(
        value, "fsdp", fsdp_perm(lambda z, x, c: (z + 1 - 2 * c, x, c))
    )


def along_x(value):
    return lax.ppermute(value, "fsdp", fsdp_perm(lambda z, x, c: (z, 1 - x, c)))


def to_core(value):
    return lax.ppermute(value, "fsdp", fsdp_perm(lambda z, x, c: (z, x, 1 - c)))


def across_replicas(value, move):
    pairs = []
    for y in range(Y):
        for x in range(XL):
            to_y, to_x = move(y, x)
            pairs.append((y * XL + x, (to_y % Y) * XL + to_x))
    return lax.ppermute(value, "replica", pairs)


def cost(flops, nbytes):
    return pl.CostEstimate(flops=flops, bytes_accessed=nbytes, transcendentals=0)


def prepare_kernel(
    gain_hbm, next_hbm, weights_hbm, out_ref, low_ref, high_ref, *refs
):
    slice_refs, (gain_ref, next_ref, sems, slice_sems) = refs[:Y], refs[Y:]
    rows = next_ref.shape[0]
    side = BLOCK
    first = pl.multiple_of(lax.axis_index("fsdp") * rows, rows)
    copies = [
        pltpu.make_async_copy(
            gain_hbm.at[:, pl.ds(first, rows)], gain_ref, sems.at[rows // side]
        )
    ]
    for i in range(rows // side):
        at = slice(i * side, (i + 1) * side)
        copies.append(
            pltpu.make_async_copy(next_hbm.at[0, at, :], next_ref.at[at, :], sems.at[i])
        )
    y = lax.axis_index("replica") // XL
    width = slice_refs[0].shape[1]
    slice_copies = []
    for dy, slice_ref in enumerate(slice_refs):
        at = pl.multiple_of(((y + dy) % Y) * width, width)
        slice_copies.append(
            pltpu.make_async_copy(
                weights_hbm.at[0, :, pl.ds(at, width)], slice_ref, slice_sems.at[dy]
            )
        )
    for copy in copies + slice_copies:
        copy.start()
    eye = lax.broadcasted_iota(jnp.int32, (side, side), 0) == lax.broadcasted_iota(
        jnp.int32, (side, side), 1
    )
    copies[0].wait()
    for i in range(rows // side):
        at = slice(i * side, (i + 1) * side)
        gain = jnp.where(eye, gain_ref[:, at], 0.0)
        column = jnp.sum(gain, axis=1, keepdims=True)
        copies[1 + i].wait()
        block = (next_ref[at, :].astype(jnp.float32) * column).astype(jnp.bfloat16)
        out_ref[at, :] = block
        if i * side < rows // 2:
            low_ref[at, :] = block
        else:
            high_ref[i * side - rows // 2 : (i + 1) * side - rows // 2, :] = block
    for copy in slice_copies:
        copy.wait()


def prepare(gain, next_weights, weights):
    _, rows, columns = next_weights.shape
    hbm = pl.BlockSpec(memory_space=pltpu.HBM)
    shapes = [(rows, columns), (rows // 2, columns), (rows // 2, columns)]
    shapes += [(rows, columns // Y)] * Y
    operands = [gain, next_weights, weights]
    return pl.pallas_call(
        prepare_kernel,
        in_specs=[hbm] * 3,
        out_specs=[pl.BlockSpec(memory_space=pltpu.VMEM)] * len(shapes),
        out_shape=[jax.ShapeDtypeStruct(s, jnp.bfloat16) for s in shapes],
        scratch_shapes=[
            pltpu.VMEM((1, rows), jnp.float32),
            pltpu.VMEM((rows, columns), jnp.bfloat16),
            pltpu.SemaphoreType.DMA((rows // BLOCK + 1,)),
            pltpu.SemaphoreType.DMA((Y,)),
        ],
        compiler_params=pltpu.CompilerParams(vmem_limit_bytes=4 * MIB),
        cost_estimate=cost(rows * columns, 4 * rows * columns),
        name="prepare",
    )(*(pltpu.with_memory_space_constraint(v, pltpu.HBM) for v in operands))


def phase(values, after=()):
    spec = pl.BlockSpec(memory_space=pl.ANY)
    count = len(values)
    return pl.pallas_call(
        lambda *refs: None,
        in_specs=[spec] * (count + len(after)),
        out_specs=[spec] * count,
        out_shape=[jax.ShapeDtypeStruct(v.shape, v.dtype) for v in values],
        input_output_aliases={i: i for i in range(count)},
        compiler_params=pltpu.CompilerParams(vmem_limit_bytes=MIB),
        cost_estimate=cost(0, 0),
        name="phase",
    )(*values, *after)


def load_kernel(tokens_hbm, tokens_ref, scale_ref, sems):
    _, rows, features = tokens_ref.shape
    parts = sems.shape[0]
    size, tile, width = rows // parts, 32, 512

    def copy(i):
        at = pl.ds(pl.multiple_of(i * size, size), size)
        return pltpu.make_async_copy(
            tokens_hbm.at[0, at, :], tokens_ref.at[0, at, :], sems.at[i]
        )

    for i in range(parts):
        copy(i).start()

    def part(i, carry):
        copy(i).wait()
        for k in range(size // tile):
            at = pl.ds(pl.multiple_of(i * size + k * tile, tile), tile)
            total = jnp.zeros((tile, width), jnp.float32)
            for j in range(features // width):
                value = tokens_ref[0, at, j * width : (j + 1) * width]
                value = value.astype(jnp.float32)
                total = total + value * value
            mean = jnp.sum(total, axis=1, keepdims=True) / features
            scale_ref[at, :] = jnp.broadcast_to(lax.rsqrt(mean + EPS), (tile, BLOCK))
        return carry

    lax.fori_loop(0, parts, part, 0)


def fetch(kernel, tokens, out_shapes, copies, name, after):
    spec = pl.BlockSpec(memory_space=pltpu.VMEM)

    def run(tokens_hbm, *refs):
        kernel(tokens_hbm, *refs[len(after) :])

    return pl.pallas_call(
        run,
        in_specs=[pl.BlockSpec(memory_space=pltpu.HBM)]
        + [pl.BlockSpec(memory_space=pl.ANY)] * len(after),
        out_specs=[spec] * len(out_shapes),
        out_shape=out_shapes,
        scratch_shapes=[pltpu.SemaphoreType.DMA((copies,))],
        compiler_params=pltpu.CompilerParams(vmem_limit_bytes=3 * MIB),
        cost_estimate=cost(tokens.size, 2 * tokens.size),
        name=name,
    )(pltpu.with_memory_space_constraint(tokens, pltpu.HBM), *after)


def project_kernel(places, rows, given, *refs):
    count = len(places)
    tokens_ref, other_tokens_ref, weight_refs = refs[0], refs[1], refs[2 : 2 + count]
    total_refs = refs[2 + count : 4 + count] if given else None
    out_ref, other_ref = refs[-2:]
    me = lax.axis_index("fsdp")
    z, x, c = me // 4, (me // 2) % 2, me % 2
    starts = []
    for step, dx, dc, first in places:
        block = ((z + (2 * c - 1) * step + Z) % Z) * 2 + (x + dx) % 2
        starts.append(pl.multiple_of((block * 2 + c) * rows + first, BLOCK))
    tile = 256

    def column(n, carry):
        at = pl.ds(pl.multiple_of(n * tile, tile), tile)
        total = total_refs[0][:, at] if given else None
        other = total_refs[1][:, at] if given else None
        for start, weight_ref in zip(starts, weight_refs):
            depth = weight_ref.shape[0]
            weight = weight_ref[:, at]
            part = jnp.dot(
                tokens_ref[0, :, pl.ds(start, depth)],
                weight,
                preferred_element_type=jnp.float32,
            )
            total = part if total is None else total + part
            part = jnp.dot(
                other_tokens_ref[0, :, pl.ds(start, depth)],
                weight,
                preferred_element_type=jnp.float32,
            )
            other = part if other is None else other + part
        out_ref[:, at] = total
        other_ref[:, at] = other.astype(other_ref.dtype)
        return carry

    lax.fori_loop(0, weight_refs[0].shape[1] // tile, column, 0)


def project(tokens, other_tokens, pieces, rows, totals=(), after=(), last=False, counted=True):
    count = tokens.shape[1]
    columns = pieces[0][1].shape[1]
    operands = [tokens, other_tokens, *(w for _, w in pieces)]
    aliases = {len(operands) + i: i for i in range(2 - last)} if totals else {}
    operands += totals
    depth = sum(w.shape[0] for _, w in pieces)
    spec = pl.BlockSpec(memory_space=pltpu.VMEM)
    places = tuple(p for p, _ in pieces)
    return pl.pallas_call(
        functools.partial(project_kernel, places, rows, bool(totals)),
        in_specs=[spec] * len(operands)
        + [pl.BlockSpec(memory_space=pl.ANY)] * len(after),
        out_specs=[spec] * 2,
        out_shape=[
            jax.ShapeDtypeStruct((count, columns), jnp.float32),
            jax.ShapeDtypeStruct(
                (count, columns), jnp.bfloat16 if last else jnp.float32
            ),
        ],
        input_output_aliases=aliases,
        compiler_params=pltpu.CompilerParams(vmem_limit_bytes=3 * MIB),
        cost_estimate=cost(4 * count * depth * columns, 2 * columns * depth)
        if counted
        else cost(1, 1),
        name="project",
    )(*operands, *after)


def finish_kernel(places, rows, given, last, *refs):
    count = len(places)
    tokens_ref, weight_refs = refs[0], refs[1 : 1 + count]
    total_refs = refs[1 + count : 1 + count + given]
    out_ref = refs[-1]
    me = lax.axis_index("fsdp")
    z, x, c = me // 4, (me // 2) % 2, me % 2
    starts = []
    for step, dx, dc, first in places:
        core = (c + dc) % 2
        shard = ((z + (2 * core - 1) * step + Z) % Z) * 4 + ((x + dx) % 2) * 2 + core
        starts.append(pl.multiple_of(shard * rows + first, BLOCK))
    tile = 512

    def column(n, carry):
        at = pl.ds(pl.multiple_of(n * tile, tile), tile)
        total = total_refs[0][:, at]
        for total_ref in total_refs[1:]:
            total = total + total_ref[:, at].astype(jnp.float32)
        for start, weight_ref in zip(starts, weight_refs):
            total = total + jnp.dot(
                tokens_ref[0, :, pl.ds(start, weight_ref.shape[0])],
                weight_ref[:, at],
                preferred_element_type=jnp.float32,
            )
        if last:
            scale_ref = refs[1 + count + given]
            out_ref[0, :, at] = (total * scale_ref[:, :1]).astype(jnp.bfloat16)
        else:
            out_ref[:, at] = total
        return carry

    lax.fori_loop(0, weight_refs[0].shape[1] // tile, column, 0)


def finish(tokens, pieces, rows, totals, row_scale=None, after=()):
    count = tokens.shape[1]
    columns = totals[0].shape[1]
    last = row_scale is not None
    operands = [tokens, *(w for _, w in pieces), *totals]
    if last:
        operands.append(row_scale)
        out_shape = jax.ShapeDtypeStruct((1, count, columns), jnp.bfloat16)
    else:
        out_shape = jax.ShapeDtypeStruct((count, columns), jnp.float32)
    depth = sum(w.shape[0] for _, w in pieces)
    spec = pl.BlockSpec(memory_space=pltpu.VMEM)
    places = tuple(p for p, _ in pieces)
    return pl.pallas_call(
        functools.partial(finish_kernel, places, rows, len(totals), last),
        in_specs=[spec] * len(operands)
        + [pl.BlockSpec(memory_space=pl.ANY)] * len(after),
        out_specs=spec,
        out_shape=out_shape,
        input_output_aliases={} if last else {1 + len(pieces): 0},
        compiler_params=pltpu.CompilerParams(vmem_limit_bytes=3 * MIB),
        cost_estimate=cost(2 * count * depth * columns, 2 * columns * depth),
        name="finish",
    )(*operands, *after)


def scale_of(values):
    target = (jnp.max(jnp.abs(values), axis=1, keepdims=True) + 1e-06) / 448.0
    high = target.astype(jnp.bfloat16).astype(jnp.float32)
    low = (target - high).astype(jnp.bfloat16).astype(jnp.float32)
    return high + low


def rounded(values):
    scale = scale_of(values)
    return (values / scale).astype(jnp.bfloat16).astype(jnp.float32) * scale


def partial_kernel(snapshot_ref, *refs):
    weight_refs, (own_ref, other_ref) = refs[:-2], refs[-2:]
    me = lax.axis_index("replica")
    y, x = me // XL, me % XL
    for dx, out_ref in ((0, own_ref), (1, other_ref)):
        column = (x + dx) % XL
        at = pl.multiple_of((y * XL + column) * BLOCK, BLOCK)
        snapshot = snapshot_ref[:, pl.ds(at, BLOCK)]
        inside = pl.ds(pl.multiple_of(column * BLOCK, BLOCK), BLOCK)
        total = None
        for weight_ref in weight_refs:
            part = rounded(snapshot - weight_ref[:, inside].astype(jnp.float32))
            total = part if total is None else total + part
        out_ref[...] = total.astype(out_ref.dtype)


def update_kernel(snapshot_ref, momentum_ref, own_ref, other_ref, new_ref, velocity_ref):
    me = lax.axis_index("replica")
    at = pl.multiple_of(me * BLOCK, BLOCK)
    snapshot = snapshot_ref[:, pl.ds(at, BLOCK)]
    average = (own_ref[...] + other_ref[...].astype(jnp.float32)) / (Y * XL)
    velocity = (DECAY * momentum_ref[...].astype(jnp.float32) + average).astype(jnp.bfloat16)
    velocity_ref[...] = velocity
    updated = snapshot - RATE * (average + DECAY * velocity.astype(jnp.float32))
    new_ref[...] = rounded(updated).astype(jnp.bfloat16)


def join_kernel(left_ref, right_ref, out_ref, copy_ref):
    width = left_ref.shape[1]
    for ref in (out_ref, copy_ref):
        ref[:, :width] = left_ref[...]
        ref[:, width:] = right_ref[...]


def join(left, right):
    rows, columns = left.shape
    out = jax.ShapeDtypeStruct((rows, 2 * columns), left.dtype)
    return whole(join_kernel, [out, out], "join", [left, right])


def assemble_kernel(*refs):
    pair_refs, (out_ref, done_ref) = refs[:-2], refs[-2:]
    me = lax.axis_index("replica")
    y, x = me // XL, me % XL
    for dy, pair_ref in enumerate(pair_refs):
        for dx in range(XL):
            owner = ((y + dy) % Y) * XL + (x + dx) % XL
            at = pl.multiple_of(owner * BLOCK, BLOCK)
            inside = slice(dx * BLOCK, (dx + 1) * BLOCK)
            out_ref[:, pl.ds(at, BLOCK)] = pair_ref[:, inside]
    done_ref[...] = jnp.zeros_like(done_ref)


def whole(kernel, out_shape, name, operands, after=()):
    spec = pl.BlockSpec(memory_space=pltpu.VMEM)
    nbytes = sum(v.size * v.dtype.itemsize for v in operands)
    count = len(operands)

    def run(*refs):
        kernel(*refs[:count], *refs[count + len(after) :])

    return pl.pallas_call(
        run,
        in_specs=[spec] * count + [pl.BlockSpec(memory_space=pl.ANY)] * len(after),
        out_specs=jax.tree.map(lambda _: spec, out_shape),
        out_shape=out_shape,
        compiler_params=pltpu.CompilerParams(vmem_limit_bytes=3 * MIB),
        cost_estimate=cost(8 * nbytes, 2 * nbytes),
        name=name,
    )(*operands, *after)


def body(tokens, gain, next_weights, weights, snapshot, momentum):
    shape = jax.ShapeDtypeStruct
    _, rows, columns = next_weights.shape
    half = rows // 2

    own, own_low, own_high, *slices = prepare(gain, next_weights, weights)

    def project_on(totals, pieces, after=(), last=False, counted=True):
        return project(
            tokens, other_tokens, pieces, rows, totals, after, last, counted
        )

    other_tokens = to_core(tokens)
    ring_1 = along_z(own)
    low_0 = along_x(own_low)
    arrived_1 = across_replicas(slices[1], lambda y, x: (y + 1, x))
    arrived_3 = across_replicas(slices[3], lambda y, x: (y - 1, x))
    tokens, row_scale = fetch(
        load_kernel,
        tokens,
        [shape(tokens.shape, tokens.dtype), shape((tokens.shape[1], BLOCK), jnp.float32)],
        12,
        "load",
        [own],
    )
    ring_1, low_0, own_high, slice_2 = phase(
        [ring_1, low_0, own_high, slices[2]], after=[row_scale, arrived_1, arrived_3]
    )

    ring_2 = along_z(ring_1)
    high_0 = along_x(own_high)
    low_1 = along_z(low_0)
    arrived_2 = across_replicas(slice_2, lambda y, x: (y + 2, x))
    totals = project_on((), [((0, 0, 0, 0), own), ((1, 0, 0, 0), ring_1)])
    own_sum, other_sum = whole(
        partial_kernel,
        [shape((rows, BLOCK), jnp.float32), shape((rows, BLOCK), jnp.bfloat16)],
        "partial",
        [snapshot, slices[0], arrived_1, arrived_2, arrived_3],
        after=[totals[0]],
    )
    other_sum = across_replicas(other_sum, lambda y, x: (y, 1 - x))
    ring_2, high_0 = phase([ring_2, high_0], after=[own_sum])

    high_r2 = ring_2[half:]
    high_r3 = along_z(high_r2)
    low_r3 = along_z(ring_2[:half])
    high_2 = along_x(high_r2)
    low_1, other_sum = phase([low_1, other_sum], after=[ring_2])

    low_2 = along_z(low_1)
    new, velocity = whole(
        update_kernel,
        [shape((rows, BLOCK), jnp.bfloat16)] * 2,
        "update",
        [snapshot, momentum, own_sum, other_sum],
    )
    new_other = across_replicas(new, lambda y, x: (y, 1 - x))
    totals = project_on(
        totals,
        [
            ((2, 0, 0, 0), ring_2),
            ((0, 1, 0, 0), low_0),
            ((0, 1, 0, half), high_0),
        ],
        after=[new],
        counted=False,
    )
    high_r3, high_0 = phase([high_r3, high_0], after=[totals[0]])

    high_3 = along_x(high_r3)
    high_1 = along_z(high_0)
    (new_other,) = phase([new_other], after=[high_r3, low_r3, high_2])
    pair, pair_sent = join(new, new_other)
    pair_1 = across_replicas(pair, lambda y, x: (y - 1, x))
    pair_3 = across_replicas(pair, lambda y, x: (y + 1, x))
    (low_2,) = phase([low_2], after=[pair])

    low_3 = along_z(low_2)
    totals = project_on(
        totals,
        [
            ((3, 0, 0, 0), low_r3),
            ((3, 0, 0, half), high_r3),
            ((1, 1, 0, 0), low_1),
        ],
        after=[low_2],
        counted=False,
    )
    (pair_sent,) = phase([pair_sent], after=[totals[0], pair_1])
    pair_2 = across_replicas(pair_sent, lambda y, x: (y + 2, x))
    own_total, other_total = project_on(
        totals,
        [
            ((2, 1, 0, half), high_2),
            ((2, 1, 0, 0), low_2),
            ((1, 1, 0, half), high_1),
            ((3, 1, 0, half), high_3),
        ],
        last=True,
        counted=False,
        after=[pair_sent],
    )
    low_3, other_total, pair_2 = phase([low_3, other_total, pair_2], after=[pair_3])

    low_3_other = to_core(low_3)
    other_total = to_core(other_total)
    own_total = finish(
        tokens, [((3, 1, 0, 0), low_3)], rows, [own_total]
    )
    new_weights, done = whole(
        assemble_kernel,
        [shape((rows, columns), jnp.bfloat16), shape((8, BLOCK), jnp.float32)],
        "assemble",
        [pair, pair_1, pair_2, pair_3],
        after=[own_total],
    )
    next_keys = finish(
        tokens,
        [((3, 1, 1, 0), low_3_other)],
        rows,
        [own_total, other_total],
        row_scale,
        after=[done],
    )
    return (next_keys, new_weights, velocity)


def solution(mesh):
    placed = (
        P("replica", "fsdp", None),
        P("replica", None),
        P("replica", "fsdp", None),
        P("replica", "fsdp", None),
        P("fsdp", None),
        P("fsdp", "replica"),
    )
    return jax.shard_map(
        body,
        mesh=mesh,
        in_specs=placed,
        out_specs=(P("replica", "fsdp", None), P("fsdp", None), P("fsdp", "replica")),
        check_vma=False,
    )
```
